128 devices in a mesh: row: 16 (over x, y_hi, core), col: 8 (over y_lo, z).
Axes of the slice: x: 4, y: 4 (y_hi: 2, y_lo: 2; y = y_hi * 2 + y_lo), z: 4, core: 2. Of those that a mesh axis runs over, the one named last changes fastest.
Arguments:
- hamiltonian: bfloat16 [8192, 8192], P('row', 'col'), may hold values from -12 to 12, as said below
- density: bfloat16 [8192, 8192], P('row', 'col'), may hold values from -0.26516504 to 0.26516504, as said below
- h_flags: int32 [128, 128], P('row', 'col'), may hold values from 0 to 1, as said below
- p_flags: int32 [128, 128], P('row', 'col'), may hold values from 0 to 1, as said below
- q_flags: int32 [128, 128], P('row', 'col'), may hold values 0 or 1
- r_flags: int32 [128, 128], P('row', 'col'), may hold values 0 or 1
Outputs:
- gradient: float32 [8192, 8192], P(('row', 'col'))
The draws below stay inside these ranges and needn't reach their ends.
Inputs may be any that keep to these rules, and one draw needn't show every extreme that they name: `h_flags`: symmetric; every diagonal block is occupied. `p_flags`: symmetric; every diagonal block is occupied. `hamiltonian`: symmetric. `density`: symmetric.
All inputs are finite; a program needn't handle non-finite values. No bound on the sum of `q_flags` or of `r_flags` on one device may be relied on, other than what follows from the above.
Results may differ from the reference program's by a relative error of at most 0.0029.
Values may be sent and summed in bfloat16 or wider, within the bound.
A program may use at most 128 MiB of HBM per device.

```python
import math
import jax
import jax.numpy as jnp
from jax import lax

B = 64
NB = 128
ORDER = 8192


def sparse_pattern(key):
    level_key, cell_key = jax.random.split(key)
    levels = jax.random.randint(level_key, (NB, 1), 1, 5)
    cells = jax.random.randint(cell_key, (NB, NB), 0, 8)
    marks = (cells < levels).astype(jnp.int32)
    marks = jnp.maximum(marks, marks.T)
    ident = (lax_iota_rows() == lax_iota_cols()).astype(jnp.int32)
    return jnp.maximum(marks, ident).astype(jnp.int32)


def lax_iota_rows():
    return jnp.arange(NB, dtype=jnp.int32)[:, None]


def lax_iota_cols():
    return jnp.arange(NB, dtype=jnp.int32)[None, :]


def draw_h_flags(key, part):
    key = jax.random.fold_in(key, 1)
    return sparse_pattern(key)


def draw_p_flags(key, part):
    key = jax.random.fold_in(key, 2)
    return sparse_pattern(key)


def symmetric_values(base, factor):
    return ((base + base.T) * 0.70710678 * factor).astype(jnp.bfloat16)


def draw_hamiltonian(key, part):
    key = jax.random.fold_in(key, 3)
    base_key = jax.random.fold_in(key, 0)
    base = jnp.clip(jax.random.normal(base_key, (ORDER, ORDER), jnp.float32), -4.0, 4.0)
    return symmetric_values(base, 1.0)


def draw_density(key, part):
    key = jax.random.fold_in(key, 4)
    base_key = jax.random.fold_in(key, 0)
    base = jnp.clip(jax.random.normal(base_key, (ORDER, ORDER), jnp.float32), -4.0, 4.0)
    return symmetric_values(base, 2.0 / math.sqrt(ORDER))


def plant(array, stream_key, least, largest):
    spot = [jax.random.randint(jax.random.fold_in(stream_key, axis), (), 0, length) for axis, length in enumerate(array.shape)]
    main_axis = array.shape.index(max(array.shape))
    next_to = spot[:main_axis] + [(spot[main_axis] + 1) % array.shape[main_axis]] + spot[main_axis + 1:]
    return array.at[tuple(spot)].set(least).at[tuple(next_to)].set(largest)


def setup_inputs(seed: int = 0) -> dict:
    key_list = jax.random.split(jax.random.key(seed), 7)
    hamiltonian = draw_hamiltonian(jax.random.fold_in(key_list[6], 71), 0)
    density = draw_density(jax.random.fold_in(key_list[6], 71), 0)
    h_flags = draw_h_flags(jax.random.fold_in(key_list[6], 71), 0)
    p_flags = draw_p_flags(jax.random.fold_in(key_list[6], 71), 0)
    q_flags = plant((jax.random.randint(key_list[4], (NB, NB), 0, 2) < 1).astype(jnp.int32), jax.random.fold_in(key_list[4], 1), 0, 1)
    r_flags = plant((jax.random.randint(key_list[5], (NB, NB), 0, 2) < 1).astype(jnp.int32), jax.random.fold_in(key_list[5], 1), 0, 1)
    return {"hamiltonian": hamiltonian, "density": density, "h_flags": h_flags, "p_flags": p_flags, "q_flags": q_flags, "r_flags": r_flags}


def blockmask(matrix, flags):
    count = flags.shape[0]
    shaped = matrix.reshape(count, B, count, B)
    return (shaped * flags.astype(matrix.dtype)[:, None, :, None]).reshape(matrix.shape)


def product(left, right):
    return jnp.dot(left.astype(jnp.float32), right.astype(jnp.float32), precision=lax.Precision.HIGHEST)


def reference(hamiltonian, density, h_flags, p_flags, q_flags, r_flags):
    h_masked = blockmask(hamiltonian, h_flags)
    p_masked = blockmask(density, p_flags)
    first = blockmask(product(h_masked, p_masked), q_flags).astype(jnp.bfloat16)
    second = blockmask(product(p_masked, first), r_flags)
    first_wide = first.astype(jnp.float32)
    return first_wide + first.T.astype(jnp.float32) - 2.0 * second
```

```python
import functools

import jax
import jax.numpy as jnp
from jax import lax
from jax.experimental import pallas as pl
from jax.experimental.pallas import tpu as pltpu
from jax.sharding import PartitionSpec as P

MESH = pl.DeviceIdType.MESH
BF = jnp.bfloat16
F32 = jnp.float32
B = 64
T = 512


def dev(x, y, z, k):
    return (x * 4 + (y // 2) * 2 + k, (y % 2) * 4 + z)


def kernel(
    ham, den, flags, out,
    ps, hs, fs, pm, hm, acc, fb, ft, gs, qv, rv, qmask, rmask, rexp,
    p_send, p_recv, h_send, h_recv, f_send, f_recv, s_send, s_recv, o_send, o_recv,
):
    row, col = lax.axis_index("row"), lax.axis_index("col")
    x, yh, k = row // 4, (row // 2) % 2, row % 2
    yl, z = col // 4, col % 4
    y = yh * 2 + yl
    zh, zl = z // 2, z % 2
    me = x * 4 + y
    source_z = 2 * (x % 2) + yh

    def near(axis, step):
        if axis == "x":
            return dev((x + step) % 4, y, z, k)
        if axis == "y":
            return dev(x, (y + step) % 4, z, k)
        return dev(x, y, (z + step) % 4, k)

    core = dev(x, y, z, 1 - k)
    diagonal = dev(x, yh * 2 + 1 - yl, z, 1 - k)
    beside = dev(x, yh * 2 + 1 - yl, z, k)

    def remote(src, dst, send, recv, device):
        return pltpu.make_async_remote_copy(
            src_ref=src, dst_ref=dst, send_sem=send, recv_sem=recv,
            device_id=device, device_id_type=MESH,
        )

    barrier = pltpu.get_barrier_semaphore()

    def greet(device):
        pl.semaphore_signal(barrier, inc=1, device_id=device, device_id_type=MESH)

    for axis in "xyz":
        for step in (1, -1):
            greet(near(axis, step))
    greet(core)
    greet(diagonal)

    def scatter_source(j):
        return dev(2 * zl + 1 - zh, 2 * k + j, source_z, yl)

    for j in (0, 1):
        greet(scatter_source(j))
    on_way = (x % 2 == zh) & (yh == zl)

    def greet_out(g, carry):
        @pl.when(jnp.logical_not(on_way & (g == me)))
        def _():
            greet(dev(g // 4, g % 4, source_z, k))
        return carry

    lax.fori_loop(0, 16, greet_out, 0)

    def spread(first):
        blocks = lax.broadcasted_iota(jnp.int32, (128, T), 0)
        places = lax.broadcasted_iota(jnp.int32, (128, T), 1) // B
        return (blocks == places + first).astype(F32)

    for half in (0, 1):
        wide = spread(8 * half)
        h_wide = jnp.dot(flags[0], wide, preferred_element_type=F32)
        p_wide = jnp.dot(flags[1], wide, preferred_element_type=F32)
        for i in range(8):
            rows, columns = pl.ds(i * B, B), pl.ds(half * T, T)
            hm[rows, columns] = (ham[rows, columns].astype(F32) * h_wide[i : i + 1]).astype(BF)
            pm[half, rows, :] = (den[rows, columns].astype(F32) * p_wide[i : i + 1]).astype(BF)
    slot_q = 2 * k + yl
    qv[slot_q] = flags[2]
    acc[...] = jnp.zeros_like(acc)

    pl.semaphore_wait(barrier, 26 - on_way.astype(jnp.int32))

    pending = []

    def go(copy):
        copy.start()
        pending.append(copy)

    p_own = pltpu.make_async_copy(pm.at[k], ps.at[me, pl.ds(k * T, T)], p_recv.at[40])
    p_own.start()
    p_swap = remote(pm.at[1 - k], ps.at[me, pl.ds(k * T, T)], p_send.at[41], p_recv.at[41], core)
    go(p_swap)

    @pl.when(k == yl)
    def _():
        pltpu.make_async_copy(hm, hs.at[4 * k + z], h_recv.at[8]).start()

    h_swap = remote(hm, hs.at[4 * (1 - k) + z], h_send.at[8], h_recv.at[8], diagonal)

    @pl.when(k != yl)
    def _():
        h_swap.start()

    go(remote(qv.at[slot_q], qv.at[slot_q], s_send.at[0], s_recv.at[0], core))
    go(remote(qv.at[slot_q], qv.at[slot_q], s_send.at[1], s_recv.at[1], diagonal))
    go(remote(qv.at[slot_q], qv.at[slot_q], s_send.at[2], s_recv.at[2], beside))
    r_local = []
    for side in (0, 1):
        tx, ty, tz = 2 * yl + zh, 2 * zl + side, source_z
        own = (tx == x) & (ty == y) & (tz == z)
        copy = remote(flags.at[3], rv.at[x // 2], s_send.at[3 + side], s_recv.at[3 + x // 2], dev(tx, ty, tz, k))
        pl.when(jnp.logical_not(own))(copy.start)
        local = pltpu.make_async_copy(flags.at[3], rv.at[x // 2], s_recv.at[3 + x // 2])
        pl.when(own)(local.start)
        r_local.append((own, copy))

    def got(dst, recv):
        remote(dst, dst, s_send.at[0], recv, core).wait_recv()

    def slot(dx, dy):
        return ((x + dx) % 4) * 4 + (y + dy) % 4

    def place(h, a, b):
        return slot(a, b) if h == 0 else slot(b, a)

    def p_part(h, a, b, part):
        first, size = (h * T, T) if part is None else (h * T + part * 256, 256)
        return ps.at[place(h, a, b), pl.ds(first, size)]

    def p_go(h, a, b, part, axis, step, index):
        ref = p_part(h, a, b, part)
        go(remote(ref, ref, p_send.at[index], p_recv.at[index], near(axis, step)))

    def p_got(h, a, b, part, index):
        got(p_part(h, a, b, part), p_recv.at[index])

    AXES = (("x", "y"), ("y", "x"))
    OFFSET = (0, -1, 1, 2)

    def first_start(h):
        p_go(h, 0, 0, None, AXES[h][0], 1, 20 * h)
        p_go(h, 0, 0, None, AXES[h][0], -1, 20 * h + 1)

    def first_pass(h):
        p_got(h, -1, 0, None, 20 * h)
        p_go(h, -1, 0, 0, AXES[h][0], 1, 20 * h + 2)
        p_got(h, 1, 0, None, 20 * h + 1)
        p_go(h, 1, 0, 1, AXES[h][0], -1, 20 * h + 3)

    def first_end(h):
        p_got(h, 2, 0, 0, 20 * h + 2)
        p_got(h, 2, 0, 1, 20 * h + 3)

    def second_start(h, j):
        base = 20 * h + 4 + 4 * j
        p_go(h, OFFSET[j], 0, None, AXES[h][1], 1, base)
        p_go(h, OFFSET[j], 0, None, AXES[h][1], -1, base + 1)

    def second_pass(h, j):
        base = 20 * h + 4 + 4 * j
        p_got(h, OFFSET[j], -1, None, base)
        p_go(h, OFFSET[j], -1, 0, AXES[h][1], 1, base + 2)
        p_got(h, OFFSET[j], 1, None, base + 1)
        p_go(h, OFFSET[j], 1, 1, AXES[h][1], -1, base + 3)

    def second_end(h, j):
        base = 20 * h + 4 + 4 * j
        p_got(h, OFFSET[j], 2, 0, base + 2)
        p_got(h, OFFSET[j], 2, 1, base + 3)

    def multiply(places):
        def add(dx, dy):
            s = slot(dx, dy)
            acc[s % 2] += jnp.dot(hs[s // 2], ps[s], preferred_element_type=F32)

        if len(places) == 1:
            add(*places[0])
            return

        def body(n, carry):
            dx = sum(jnp.where(n == i, p[0], 0) for i, p in enumerate(places))
            dy = sum(jnp.where(n == i, p[1], 0) for i, p in enumerate(places))
            add(dx, dy)
            return carry

        lax.fori_loop(0, len(places), body, 0)

    p_own.wait()
    got(ps.at[me, pl.ds((1 - k) * T, T)], p_recv.at[41])
    for h in (0, 1):
        first_start(h)
    for h in (0, 1):
        second_start(h, 0)

    h_home = 4 * k + z
    got(hs.at[h_home], h_recv.at[8])

    def h_slot(step, c):
        return 4 * c + (z + step) % 4

    def h_go(step, part, way, index):
        ref = hs.at[h_slot(step, k)] if part is None else hs.at[h_slot(step, k), pl.ds(part * 256, 256)]
        go(remote(ref, ref, h_send.at[index], h_recv.at[index], near("z", way)))

    def h_got(step, part, index):
        ref = hs.at[h_slot(step, k)] if part is None else hs.at[h_slot(step, k), pl.ds(part * 256, 256)]
        got(ref, h_recv.at[index])

    def h_share(step, index):
        ref = hs.at[h_slot(step, k)]
        go(remote(ref, ref, h_send.at[index], h_recv.at[index], core))

    h_go(0, None, 1, 0)
    h_go(0, None, -1, 1)
    h_share(0, 4)

    for h in (0, 1):
        first_pass(h)
        second_start(h, 1)
        second_start(h, 2)
    for n, place_q in enumerate((2 * (1 - k) + yl, 2 * (1 - k) + 1 - yl, 2 * k + 1 - yl)):
        got(qv.at[place_q], s_recv.at[n])
    for n in range(2):
        got(rv.at[n], s_recv.at[3 + n])
    narrow = spread(8 * k)
    for c in (0, 1):
        q_wide = jnp.dot(qv[2 * yl + c], narrow, preferred_element_type=F32)
        for i in range(8):
            qmask[c, pl.ds(i * B, B), :] = jnp.broadcast_to(q_wide[i : i + 1], (B, T)).astype(BF)
        eight = (lax.broadcasted_iota(jnp.int32, (8, T), 0) == lax.broadcasted_iota(jnp.int32, (8, T), 1) // B)
        rexp[...] = lax.dot_general(rv[c], eight.astype(F32), (((0,), (0,)), ((), ())), preferred_element_type=F32)
        r_wide = rexp[pl.ds(pl.multiple_of(yl * 8, 8), 8), :]
        for i in range(8):
            rmask[c, pl.ds(i * B, B), :] = jnp.broadcast_to(2.0 * r_wide[i : i + 1], (B, T)).astype(BF)

    for h in (0, 1):
        second_pass(h, 0)
    h_got(-1, None, 0)
    h_go(-1, 0, 1, 2)
    h_share(-1, 5)
    h_got(1, None, 1)
    h_go(1, 1, -1, 3)
    h_share(1, 6)
    for h in (0, 1):
        first_end(h)
        second_start(h, 3)
    for h in (0, 1):
        second_end(h, 0)
    h_got(2, 0, 2)
    h_got(2, 1, 3)
    h_share(2, 7)
    for h in (0, 1):
        second_pass(h, 1)
        second_pass(h, 2)
    for n, step in enumerate((0, -1, 1, 2)):
        got(hs.at[h_slot(step, 1 - k)], h_recv.at[4 + n])
    multiply([(0, 0), (1, 0), (-1, 0), (0, 1), (0, -1), (2, 0), (0, 2), (1, 1), (1, -1), (-1, 1), (-1, -1)])
    for h in (0, 1):
        second_pass(h, 3)
    for h in (0, 1):
        second_end(h, 1)
        second_end(h, 2)
    multiply([(2, 1), (2, -1), (1, 2), (-1, 2)])
    for h in (0, 1):
        second_end(h, 3)
    multiply([(2, 2)])

    for c in (0, 1):
        first = acc[c] * qmask[c].astype(F32)
        fb[c] = first.astype(BF)
        ft[c] = first.T.astype(BF)
        target = dev(2 * c + zh, 2 * zl + k, 2 * (1 - x % 2) + x // 2, yh)
        go(remote(ft.at[c], fs.at[me], f_send.at[c], f_recv.at[yl], target))
        acc[c] = jnp.zeros((T, T), F32)

    def f_slot(step, c, j):
        zz = (z + step) % 4
        return (2 * (zz % 2) + 1 - zz // 2) * 4 + 2 * c + j

    def f_go(step, j, device, index):
        ref = fs.at[f_slot(step, k, j)]
        go(remote(ref, ref, f_send.at[index], f_recv.at[index], device))

    def f_got(step, c, j, index):
        got(fs.at[f_slot(step, c, j)], f_recv.at[index])

    def multiply_second(n, fn):
        def body(i, carry):
            step, c = fn(i)
            zz = (z + step) % 4
            xs = 2 * (zz % 2) + 1 - zz // 2
            for j in (0, 1):
                for half in (0, 1):
                    acc[half] += jnp.dot(
                        fs[xs * 4 + 2 * c + j], ps[xs * 4 + 2 * c + half, pl.ds(j * T, T), :],
                        preferred_element_type=F32,
                    )
            return carry

        lax.fori_loop(0, n, body, 0)

    for j in (0, 1):
        f_got(0, k, j, j)
        f_go(0, j, near("z", 1), 2 + j)
        f_go(0, j, near("z", -1), 4 + j)
        f_go(0, j, core, 8 + j)
    multiply_second(1, lambda i: (0, k))
    for j in (0, 1):
        f_got(-1, k, j, 2 + j)
        if j == 0:
            f_go(-1, 0, near("z", 1), 6)
        f_go(-1, j, core, 10 + j)
        f_got(1, k, j, 4 + j)
        if j == 1:
            f_go(1, 1, near("z", -1), 7)
        f_go(1, j, core, 12 + j)
    for j in (0, 1):
        f_got(0, 1 - k, j, 8 + j)
    multiply_second(3, lambda i: (jnp.where(i == 0, 0, 2 * i - 3), jnp.where(i == 0, 1 - k, k)))
    for j in (0, 1):
        f_got(2, k, j, 6 + j)
        f_go(2, j, core, 14 + j)
    for j in (0, 1):
        f_got(-1, 1 - k, j, 10 + j)
        f_got(1, 1 - k, j, 12 + j)
    multiply_second(3, lambda i: (jnp.where(i == 0, 2, 2 * i - 3), jnp.where(i == 0, k, 1 - k)))
    for j in (0, 1):
        f_got(2, 1 - k, j, 14 + j)
    multiply_second(1, lambda i: (2, 1 - k))

    o_copies = []
    for c in (0, 1):
        turned = fs[(2 * c + zh) * 4 + 2 * zl + k].astype(F32)
        value = fb[c].astype(F32) + turned - acc[c] * rmask[c].astype(F32)
        gs[c] = value.T.astype(BF)
        mine = pl.ds(pl.multiple_of(me * T, T), T)

        def send_rows(b, carry, wait=False, c=c):
            rows = gs.at[c, pl.ds(pl.multiple_of(b * B, B), B)]
            tx, ty, tz = 2 * c + zh, 2 * zl + b // 4, b % 4
            own = (tx == x) & (ty == y) & (tz == z)
            copy = remote(rows, out.at[:, mine], o_send.at[c * 8 + b], o_recv.at[me], dev(tx, ty, tz, k))
            pl.when(jnp.logical_not(own))(copy.wait_send if wait else copy.start)
            if not wait:
                pl.when(own)(pltpu.make_async_copy(rows, out.at[:, mine], o_recv.at[me]).start)
            return carry

        lax.fori_loop(0, 8, send_rows, 0)
        o_copies.append(functools.partial(send_rows, wait=True))

    def take(g, carry):
        got(out.at[:, pl.ds(pl.multiple_of(g * T, T), T)], o_recv.at[g])
        return carry

    lax.fori_loop(0, 16, take, 0)
    for copy in pending:
        copy.wait_send()
    pl.when(k != yl)(h_swap.wait_send)
    for own, copy in r_local:
        pl.when(jnp.logical_not(own))(copy.wait_send)
    for wait in o_copies:
        lax.fori_loop(0, 8, wait, 0)


def per_device(hamiltonian, density, h_flags, p_flags, q_flags, r_flags):
    flags = jnp.stack([h_flags, p_flags, q_flags, r_flags]).astype(F32)
    flags = jnp.pad(flags, ((0, 0), (0, 0), (0, 112)))
    dma = pltpu.SemaphoreType.DMA
    rows = pl.pallas_call(
        kernel,
        out_shape=jax.ShapeDtypeStruct((64, 8192), BF),
        in_specs=[pl.BlockSpec(memory_space=pltpu.VMEM)] * 3,
        out_specs=pl.BlockSpec(memory_space=pl.ANY),
        scratch_shapes=[
            pltpu.VMEM((16, 2 * T, T), BF),
            pltpu.VMEM((8, T, 2 * T), BF),
            pltpu.VMEM((16, T, T), BF),
            pltpu.VMEM((2, T, T), BF),
            pltpu.VMEM((T, 2 * T), BF),
            pltpu.VMEM((2, T, T), F32),
            pltpu.VMEM((2, T, T), BF),
            pltpu.VMEM((2, T, T), BF),
            pltpu.VMEM((2, T, T), BF),
            pltpu.VMEM((4, 8, 128), F32),
            pltpu.VMEM((2, 8, 128), F32),
            pltpu.VMEM((2, T, T), BF),
            pltpu.VMEM((2, T, T), BF),
            pltpu.VMEM((128, T), F32),
            dma((42,)), dma((42,)), dma((9,)), dma((9,)), dma((16,)), dma((16,)),
            dma((5,)), dma((5,)), dma((16,)), dma((16,)),
        ],
        compiler_params=pltpu.CompilerParams(
            collective_id=0, has_side_effects=True, vmem_limit_bytes=60 * 1024 * 1024
        ),
        cost_estimate=pl.CostEstimate(flops=2 * 2 * 512 * 8192 * 1024, bytes_accessed=4 << 20, transcendentals=0),
    )(hamiltonian, density, flags)
    return rows.astype(F32)


def solution(mesh):
    spec = P("row", "col")
    return jax.shard_map(
        per_device,
        mesh=mesh,
        in_specs=(spec,) * 6,
        out_specs=P(("row", "col"), None),
        check_vma=False,
    )
```

```python
import jax
import jax.numpy as jnp
from jax import lax
from jax.experimental import pallas as pl
from jax.experimental.pallas import tpu as pltpu
from jax.sharding import PartitionSpec as P

MESH = pl.DeviceIdType.MESH
BF = jnp.bfloat16
F32 = jnp.float32
B = 64
T = 512
U = 256


def dev(x, y, z, k):
    return (x * 4 + (y // 2) * 2 + k, (y % 2) * 4 + z)


def kernel(
    ham, den, flags, out,
    ps, hs, fs, hm, acc, sums, fb, ft, gs, qv, rv, qmask, rmask, qexp,
    p_send, p_recv, h_send, h_recv, f_send, f_recv, s_send, s_recv, o_send, o_recv,
):
    row, col = lax.axis_index("row"), lax.axis_index("col")
    x, yh, k = row // 4, (row // 2) % 2, row % 2
    yl, z = col // 4, col % 4
    y = yh * 2 + yl
    zh, zl = z // 2, z % 2
    xh, xl = x // 2, x % 2
    me = y * 4 + z
    plane = 2 * yl + zh

    def near(axis, step):
        if axis == "x":
            return dev((x + step) % 4, y, z, k)
        if axis == "y":
            return dev(x, (y + step) % 4, z, k)
        return dev(x, y, (z + step) % 4, k)

    core = dev(x, y, z, 1 - k)
    across = near("y", 2)

    def remote(src, dst, send, recv, device):
        return pltpu.make_async_remote_copy(
            src_ref=src, dst_ref=dst, send_sem=send, recv_sem=recv,
            device_id=device, device_id_type=MESH,
        )

    barrier = pltpu.get_barrier_semaphore()

    def greet(device):
        pl.semaphore_signal(barrier, inc=1, device_id=device, device_id_type=MESH)

    def greet_plane(n, carry):
        greet(dev(x, (y + n // 4) % 4, (z + n % 4) % 4, k))
        return carry

    lax.fori_loop(1, 16, greet_plane, 0)
    greet(near("x", 1))
    greet(near("x", -1))
    greet(core)
    for j in (0, 1):
        greet(dev(plane, (x + plane) % 4, 2 * (1 - k) + j, yh))
    mirror = (x == plane) & (y == 2 * k + xh) & (z == 2 * xl + yh)
    for c in (0, 1):
        pl.when(jnp.logical_not(mirror & (zl == c)))(
            lambda c=c: greet(dev(plane, 2 * zl + xh, 2 * xl + c, yh))
        )

    def spread(first):
        blocks = lax.broadcasted_iota(jnp.int32, (128, T), 0)
        places = lax.broadcasted_iota(jnp.int32, (128, T), 1) // B
        return (blocks == places + first).astype(F32)

    for half in (0, 1):
        wide = spread(8 * half)
        h_wide = jnp.dot(flags[0], wide, preferred_element_type=F32)
        p_wide = jnp.dot(flags[1], wide, preferred_element_type=F32)
        for i in range(8):
            rows, columns = pl.ds(i * B, B), pl.ds(half * T, T)
            ps[me, half, rows, :] = (den[rows, columns].astype(F32) * p_wide[i : i + 1]).astype(BF)
            hm[half, rows, :] = (ham[rows, columns].astype(F32) * h_wide[i : i + 1]).astype(BF)
    rv[yh] = flags[3]

    pl.semaphore_wait(barrier, 22 - mirror.astype(jnp.int32))

    pending = []

    def go(copy):
        copy.start()
        pending.append(copy)

    def got(dst, recv):
        remote(dst, dst, s_send.at[0], recv, core).wait_recv()

    AXES = (("y", "z"), ("z", "y"))
    OFFSET = (0, -1, 1, 2)

    def p_part(u, h, a, b, part):
        dy, dz = (a, b) if h == 0 else (b, a)
        s = ((y + dy) % 4) * 4 + (z + dz) % 4
        first, size = (u * U + h * 128, 128) if part is None else (u * U + h * 128 + part * 64, 64)
        return ps.at[s, :, pl.ds(first, size), :]

    def p_go(u, h, a, b, part, axis, step, index):
        ref = p_part(u, h, a, b, part)
        go(remote(ref, ref, p_send.at[index], p_recv.at[index], near(axis, step)))

    def p_got(u, h, a, b, part, index):
        got(p_part(u, h, a, b, part), p_recv.at[index])

    def first_start(u):
        for h in (0, 1):
            base = 40 * u + 20 * h
            p_go(u, h, 0, 0, None, AXES[h][0], 1, base)
            p_go(u, h, 0, 0, None, AXES[h][0], -1, base + 1)

    def first_pass(u):
        for h in (0, 1):
            base = 40 * u + 20 * h
            p_got(u, h, -1, 0, None, base)
            p_go(u, h, -1, 0, 0, AXES[h][0], 1, base + 2)
            p_got(u, h, 1, 0, None, base + 1)
            p_go(u, h, 1, 0, 1, AXES[h][0], -1, base + 3)

    def first_end(u):
        for h in (0, 1):
            base = 40 * u + 20 * h
            p_got(u, h, 2, 0, 0, base + 2)
            p_got(u, h, 2, 0, 1, base + 3)

    def second_start(u, j):
        for h in (0, 1):
            base = 40 * u + 20 * h + 4 + 4 * j
            p_go(u, h, OFFSET[j], 0, None, AXES[h][1], 1, base)
            p_go(u, h, OFFSET[j], 0, None, AXES[h][1], -1, base + 1)

    def second_pass(u, j):
        for h in (0, 1):
            base = 40 * u + 20 * h + 4 + 4 * j
            p_got(u, h, OFFSET[j], -1, None, base)
            p_go(u, h, OFFSET[j], -1, 0, AXES[h][1], 1, base + 2)
            p_got(u, h, OFFSET[j], 1, None, base + 1)
            p_go(u, h, OFFSET[j], 1, 1, AXES[h][1], -1, base + 3)

    def second_end(u, j):
        for h in (0, 1):
            base = 40 * u + 20 * h + 4 + 4 * j
            p_got(u, h, OFFSET[j], 2, 0, base + 2)
            p_got(u, h, OFFSET[j], 2, 1, base + 3)

    def h_part(step, c, piece=None):
        block = ((x + step) % 4) * 2
        if piece is None:
            return hs.at[pl.ds(block, 2), pl.ds(pl.multiple_of(c * T, T), T), :]
        return hs.at[block + piece, pl.ds(pl.multiple_of(c * T, T), T), :]

    def h_go(step, piece, device, index):
        ref = h_part(step, k, piece)
        go(remote(ref, ref, h_send.at[index], h_recv.at[index], device))

    def h_got(step, c, piece, index):
        got(h_part(step, c, piece), h_recv.at[index])

    def multiply(u, first, count):
        rows = pl.ds(u * U, U)

        def body(n, carry):
            s = ((y + n // 4) % 4) * 4 + (z + n % 4) % 4
            acc[s // 8, rows, :] += jnp.dot(
                ps[s, 0, rows, :], hs[s % 8, pl.ds(0, T), :], preferred_element_type=F32
            ) + jnp.dot(ps[s, 1, rows, :], hs[s % 8, pl.ds(T, T), :], preferred_element_type=F32)
            return carry

        lax.fori_loop(first, first + count, body, 0)

    def f_part(u, step, c, j=None):
        first = ((x + step + plane) % 4) * 4 + 2 * (1 - c)
        return fs.at[u, pl.ds(first, 2)] if j is None else fs.at[u, first + j]

    def f_go(u, step, j, device, index):
        ref = f_part(u, step, k, j)
        go(remote(ref, ref, f_send.at[10 * u + index], f_recv.at[10 * u + index], device))

    def f_got(u, step, c, j, index):
        got(f_part(u, step, c, j), f_recv.at[10 * u + index])

    def scatter(u):
        rows = pl.ds(u * U, U)
        for c in (0, 1):
            first = acc[c, rows, :] * qmask[c, rows, :].astype(F32)
            fb[c, rows, :] = first.astype(BF)
            ft[u, c] = first.T.astype(BF)
            target = dev((y - x) % 4, 2 * k + xh, 2 * xl + c, 1 - zh)
            go(remote(ft.at[u, c], fs.at[u, me], f_send.at[10 * u + c], f_recv.at[10 * u + zl], target))

    def ring_start(u):
        for j in (0, 1):
            f_got(u, 0, k, j, j)
        f_go(u, 0, None, near("x", 1), 2)
        f_go(u, 0, None, near("x", -1), 3)
        f_go(u, 0, None, core, 6)

    def ring_pass(u):
        f_got(u, -1, k, None, 2)
        f_go(u, -1, 0, near("x", 1), 4)
        f_go(u, -1, None, core, 7)
        f_got(u, 1, k, None, 3)
        f_go(u, 1, 1, near("x", -1), 5)
        f_go(u, 1, None, core, 8)

    def ring_end(u):
        f_got(u, 2, k, 0, 4)
        f_got(u, 2, k, 1, 5)
        f_go(u, 2, None, core, 9)

    def multiply_second(u, places):
        def body(n, carry):
            step = sum(jnp.where(n == i, p[0], 0) for i, p in enumerate(places))
            c = sum(jnp.where(n == i, p[1], 0) for i, p in enumerate(places))
            sy = (x + step + plane) % 4
            for j in (0, 1):
                sz = 2 * (1 - c) + j
                for half in (0, 1):
                    sums[half, u] += jnp.dot(
                        ps[half * 8 + (sy % 2) * 4 + sz, sy // 2], fs[u, sy * 4 + sz],
                        preferred_element_type=F32,
                    )
            return carry

        lax.fori_loop(0, len(places), body, 0)

    def columns_of(sy, sz, u):
        return pl.ds(pl.multiple_of(((sy % 2) * 4 + sz) * 2 * T + (sy // 2) * T + u * U, U), U)

    def finish(u):
        columns = pl.ds(u * U, U)
        for c in (0, 1):
            straight = fs[u, (2 * k + xh) * 4 + 2 * xl + c].astype(F32)
            value = straight + fb[c, :, columns].astype(F32) - sums[c, u] * rmask[c, :, columns].astype(F32)
            gs[c, u] = value.astype(BF)

        def rows_for(n):
            ty, tz = (y + n // 4) % 4, (z + n % 4) % 4
            b = (ty % 2) * 4 + tz
            return gs.at[ty // 2, u, pl.ds(pl.multiple_of(b * B, B), B), :], dev(x, ty, tz, k)

        mine = out.at[:, columns_of(y, z, u)]
        local = pltpu.make_async_copy(rows_for(0)[0], mine, o_recv.at[16 * u + me])
        local.start()

        def copy(n):
            rows, device = rows_for(n)
            return remote(rows, mine, o_send.at[16 * u + n], o_recv.at[16 * u + me], device)

        def start(n, carry):
            copy(n).start()
            return carry

        lax.fori_loop(1, 16, start, 0)
        return copy

    q_copies = []
    for side in (0, 1):
        own = mirror & (k == side)
        copy = remote(
            flags.at[2], qv.at[zl], s_send.at[side], s_recv.at[zl],
            dev(2 * yl + zh, 2 * k + xh, 2 * xl + yh, side),
        )
        pl.when(jnp.logical_not(own))(copy.start)
        pl.when(own)(pltpu.make_async_copy(flags.at[2], qv.at[zl], s_recv.at[zl]).start)
        q_copies.append((own, copy))
    go(remote(rv.at[yh], rv.at[yh], s_send.at[2], s_recv.at[2], across))
    home = hs.at[2 * x + yh, pl.ds(pl.multiple_of(k * T, T), T), :]
    go(remote(hm.at[1 - yh], home, h_send.at[0], h_recv.at[0], across))
    h_local = pltpu.make_async_copy(hm.at[yh], home, h_recv.at[1])
    h_local.start()

    first_start(0)
    second_start(0, 0)
    acc[...] = jnp.zeros_like(acc)
    sums[...] = jnp.zeros_like(sums)
    first_pass(0)
    second_start(0, 1)
    second_start(0, 2)

    first_start(1)
    second_start(1, 0)
    h_local.wait()
    got(hs.at[2 * x + 1 - yh, pl.ds(pl.multiple_of(k * T, T), T), :], h_recv.at[0])
    h_go(0, None, near("x", 1), 2)
    h_go(0, None, near("x", -1), 3)
    h_go(0, None, core, 6)
    second_pass(0, 0)
    first_end(0)
    second_start(0, 3)

    for n in (0, 1):
        got(qv.at[n], s_recv.at[n])
    got(rv.at[1 - yh], s_recv.at[2])
    eight = lax.broadcasted_iota(jnp.int32, (8, T), 0) == lax.broadcasted_iota(jnp.int32, (8, T), 1) // B
    narrow = spread(8 * yh)
    for c in (0, 1):
        qexp[...] = lax.dot_general(qv[c], eight.astype(F32), (((0,), (0,)), ((), ())), preferred_element_type=F32)
        q_wide = qexp[pl.ds(pl.multiple_of(k * 8, 8), 8), :]
        r_wide = 2.0 * jnp.dot(rv[c], narrow, preferred_element_type=F32)
        for i in range(8):
            qmask[c, pl.ds(i * B, B), :] = jnp.broadcast_to(q_wide[i : i + 1], (B, T)).astype(BF)
            rmask[c, pl.ds(i * B, B), :] = jnp.broadcast_to(r_wide[i : i + 1], (B, T)).astype(BF)

    second_end(0, 0)
    first_pass(1)
    second_start(1, 1)
    second_start(1, 2)
    second_pass(0, 1)
    second_pass(0, 2)
    h_got(-1, k, None, 2)
    h_go(-1, 0, near("x", 1), 4)
    h_go(-1, None, core, 7)
    h_got(1, k, None, 3)
    h_go(1, 1, near("x", -1), 5)
    h_go(1, None, core, 8)
    second_pass(1, 0)
    second_pass(0, 3)
    first_end(1)
    second_start(1, 3)
    second_end(0, 1)
    second_end(0, 2)
    h_got(2, k, 0, 4)
    h_got(2, k, 1, 5)
    h_go(2, None, core, 9)
    second_end(1, 0)
    second_end(0, 3)
    for n, step in enumerate((0, -1, 1, 2)):
        h_got(step, 1 - k, None, 6 + n)

    multiply(0, 0, 5)
    second_pass(1, 1)
    multiply(0, 5, 5)
    second_pass(1, 2)
    multiply(0, 10, 6)
    scatter(0)
    second_pass(1, 3)
    ring_start(0)
    second_end(1, 1)
    second_end(1, 2)
    ring_pass(0)
    second_end(1, 3)
    multiply(1, 0, 16)
    scatter(1)
    ring_end(0)
    multiply_second(0, [(0, k), (-1, k), (1, k)])
    ring_start(1)
    for n, step in enumerate((0, -1, 1, 2)):
        f_got(0, step, 1 - k, None, 6 + n)
    multiply_second(0, [(2, k), (0, 1 - k), (-1, 1 - k), (1, 1 - k), (2, 1 - k)])
    ring_pass(1)
    o_copy = [finish(0)]
    f_got(1, 0, 1 - k, None, 6)
    multiply_second(1, [(0, k), (-1, k), (1, k), (0, 1 - k)])
    ring_end(1)
    f_got(1, -1, 1 - k, None, 7)
    f_got(1, 1, 1 - k, None, 8)
    multiply_second(1, [(2, k), (-1, 1 - k), (1, 1 - k)])
    f_got(1, 2, 1 - k, None, 9)
    multiply_second(1, [(2, 1 - k)])
    o_copy.append(finish(1))

    for u in (0, 1):
        def take(n, carry, u=u):
            got(out.at[:, columns_of(n // 4, n % 4, u)], o_recv.at[16 * u + n])
            return carry

        lax.fori_loop(0, 16, take, 0)
    for copy in pending:
        copy.wait_send()
    for own, copy in q_copies:
        pl.when(jnp.logical_not(own))(copy.wait_send)
    for copy in o_copy:
        def sent(n, carry, copy=copy):
            copy(n).wait_send()
            return carry

        lax.fori_loop(1, 16, sent, 0)


def per_device(hamiltonian, density, h_flags, p_flags, q_flags, r_flags):
    flags = jnp.stack([h_flags, p_flags, q_flags, r_flags]).astype(F32)
    flags = jnp.pad(flags, ((0, 0), (0, 0), (0, 112)))
    dma = pltpu.SemaphoreType.DMA
    rows = pl.pallas_call(
        kernel,
        out_shape=jax.ShapeDtypeStruct((64, 8192), BF),
        in_specs=[pl.BlockSpec(memory_space=pltpu.VMEM)] * 3,
        out_specs=pl.BlockSpec(memory_space=pl.ANY),
        scratch_shapes=[
            pltpu.VMEM((16, 2, T, T), BF),
            pltpu.VMEM((8, 2 * T, T), BF),
            pltpu.VMEM((2, 16, T, U), BF),
            pltpu.VMEM((2, T, T), BF),
            pltpu.VMEM((2, T, T), F32),
            pltpu.VMEM((2, 2, T, U), F32),
            pltpu.VMEM((2, T, T), BF),
            pltpu.VMEM((2, 2, T, U), BF),
            pltpu.VMEM((2, 2, T, U), BF),
            pltpu.VMEM((2, 8, 128), F32),
            pltpu.VMEM((2, 8, 128), F32),
            pltpu.VMEM((2, T, T), BF),
            pltpu.VMEM((2, T, T), BF),
            pltpu.VMEM((128, T), F32),
            dma((80,)), dma((80,)), dma((10,)), dma((10,)), dma((20,)), dma((20,)),
            dma((3,)), dma((3,)), dma((32,)), dma((32,)),
        ],
        compiler_params=pltpu.CompilerParams(
            collective_id=0, has_side_effects=True, vmem_limit_bytes=60 * 1024 * 1024
        ),
        cost_estimate=pl.CostEstimate(flops=2 * 2 * 512 * 8192 * 1024, bytes_accessed=4 << 20, transcendentals=0),
    )(hamiltonian, density, flags)
    return rows.astype(F32)


def solution(mesh):
    spec = P("row", "col")
    return jax.shard_map(
        per_device,
        mesh=mesh,
        in_specs=(spec,) * 6,
        out_specs=P(("row", "col"), None),
        check_vma=False,
    )
```

```python
import jax
import jax.numpy as jnp
from jax import lax
from jax.experimental import pallas as pl
from jax.experimental.pallas import tpu as pltpu
from jax.sharding import PartitionSpec as P

MESH = pl.DeviceIdType.MESH
BF = jnp.bfloat16
F32 = jnp.float32
B = 64
T = 512
PARTS = ((0, 256), (256, 128), (384, 128))
STREAMS = (((0, 160), (160, 96)), ((256, 64), (320, 64)), ((384, 64), (448, 64)))
N = len(PARTS)


def dev(x, y, z, k):
    return (x * 4 + (y // 2) * 2 + k, (y % 2) * 4 + z)


def kernel(
    ham, den, flags, out,
    ps, hs, fs, hm, acc, sums, fb, ft, gs, qv, rv, qmask, rmask, qexp,
    p_send, p_recv, h_send, h_recv, f_send, f_recv, s_send, s_recv, o_send, o_recv,
):
    row, col = lax.axis_index("row"), lax.axis_index("col")
    x, yh, k = row // 4, (row // 2) % 2, row % 2
    yl, z = col // 4, col % 4
    y = yh * 2 + yl
    zh, zl = z // 2, z % 2
    xh, xl = x // 2, x % 2
    me = y * 4 + z
    plane = 2 * yl + zh

    def near(axis, step):
        if axis == "x":
            return dev((x + step) % 4, y, z, k)
        if axis == "y":
            return dev(x, (y + step) % 4, z, k)
        return dev(x, y, (z + step) % 4, k)

    core = dev(x, y, z, 1 - k)
    across = near("y", 2)

    def remote(src, dst, send, recv, device):
        return pltpu.make_async_remote_copy(
            src_ref=src, dst_ref=dst, send_sem=send, recv_sem=recv,
            device_id=device, device_id_type=MESH,
        )

    barrier = pltpu.get_barrier_semaphore()

    def greet(device):
        pl.semaphore_signal(barrier, inc=1, device_id=device, device_id_type=MESH)

    def greet_plane(n, carry):
        greet(dev(x, (y + n // 4) % 4, (z + n % 4) % 4, k))
        return carry

    lax.fori_loop(1, 16, greet_plane, 0)
    greet(near("x", 1))
    greet(near("x", -1))
    greet(core)
    for j in (0, 1):
        greet(dev(plane, (x + plane) % 4, 2 * (1 - k) + j, yh))
    mirror = (x == plane) & (y == 2 * k + xh) & (z == 2 * xl + yh)
    for c in (0, 1):
        pl.when(jnp.logical_not(mirror & (zl == c)))(
            lambda c=c: greet(dev(plane, 2 * zl + xh, 2 * xl + c, yh))
        )

    def spread(first):
        blocks = lax.broadcasted_iota(jnp.int32, (128, T), 0)
        places = lax.broadcasted_iota(jnp.int32, (128, T), 1) // B
        return (blocks == places + first).astype(F32)

    wides = [spread(8 * half) for half in (0, 1)]

    def masked(matrix, which, half, i):
        wide = jnp.dot(flags[which], wides[half], preferred_element_type=F32)
        return (matrix[pl.ds(i * B, B), pl.ds(half * T, T)].astype(F32) * wide[i : i + 1]).astype(BF)

    for half in (0, 1):
        for i in range(8):
            ps[me, half, pl.ds(i * B, B), :] = masked(den, 1, half, i)

    pl.semaphore_wait(barrier, 22 - mirror.astype(jnp.int32))

    pending = []

    def go(copy):
        copy.start()
        pending.append(copy)

    def got(dst, recv):
        remote(dst, dst, s_send.at[0], recv, core).wait_recv()

    AXES = (("y", "z"), ("z", "y"))
    OFFSET = (0, -1, 1, 2)

    def p_part(u, h, a, b, part):
        dy, dz = (a, b) if h == 0 else (b, a)
        s = ((y + dy) % 4) * 4 + (z + dz) % 4
        first, size = STREAMS[u][h]
        if part is not None:
            first, size = first + part * (size // 2), size // 2
        return ps.at[s, :, pl.ds(first, size), :]

    def p_go(u, h, a, b, part, axis, step, index):
        ref = p_part(u, h, a, b, part)
        go(remote(ref, ref, p_send.at[index], p_recv.at[index], near(axis, step)))

    def p_got(u, h, a, b, part, index):
        got(p_part(u, h, a, b, part), p_recv.at[index])

    def own(u, h):
        base = 40 * u + 20 * h
        p_go(u, h, 0, 0, None, AXES[h][0], 1, base)
        p_go(u, h, 0, 0, None, AXES[h][0], -1, base + 1)

    def pass_first(u, h, d):
        base, step = 40 * u + 20 * h, 1 - 2 * d
        p_got(u, h, -step, 0, None, base + d)
        p_go(u, h, -step, 0, d, AXES[h][0], step, base + 2 + d)

    def turn(u, h, j):
        base = 40 * u + 20 * h
        if j == 3:
            p_got(u, h, 2, 0, 0, base + 2)
            p_got(u, h, 2, 0, 1, base + 3)
        base += 4 + 4 * j
        p_go(u, h, OFFSET[j], 0, None, AXES[h][1], 1, base)
        p_go(u, h, OFFSET[j], 0, None, AXES[h][1], -1, base + 1)

    def pass_second(u, h, j, d):
        base, step = 40 * u + 20 * h + 4 + 4 * j, 1 - 2 * d
        p_got(u, h, OFFSET[j], -step, None, base + d)
        p_go(u, h, OFFSET[j], -step, d, AXES[h][1], step, base + 2 + d)

    def p_end(u, j):
        for h in (0, 1):
            base = 40 * u + 20 * h + 4 + 4 * j
            p_got(u, h, OFFSET[j], 2, 0, base + 2)
            p_got(u, h, OFFSET[j], 2, 1, base + 3)

    def h_part(step, c, p, part=None):
        first, size = (0, T) if part is None else (part * 256, 256)
        rows = pl.ds(pl.multiple_of(c * T + first, 256), size)
        return hs.at[((x + step) % 4) * 2 + (yh if p == 0 else 1 - yh), rows, :]

    def h_go(step, p, part, device, index):
        ref = h_part(step, k, p, part)
        go(remote(ref, ref, h_send.at[10 * p + index], h_recv.at[10 * p + index], device))

    def h_got(step, c, p, part, index):
        got(h_part(step, c, p, part), h_recv.at[10 * p + index])

    def h_swap():
        for half in (0, 1):
            for i in range(8):
                hm[half, pl.ds(i * B, B), :] = masked(ham, 0, half, i)
        go(remote(hm.at[1 - yh], h_part(0, k, 0), h_send.at[10], h_recv.at[10], across))
        h_local = pltpu.make_async_copy(hm.at[yh], h_part(0, k, 0), h_recv.at[0])
        h_local.start()
        h_local.wait()

    def h_start(p):
        if p == 1:
            h_got(0, k, 1, None, 0)
        h_go(0, p, None, near("x", 1), 2)
        h_go(0, p, None, near("x", -1), 3)
        h_go(0, p, None, core, 6)

    def h_pass(p, d):
        step = 1 - 2 * d
        h_got(-step, k, p, None, 2 + d)
        h_go(-step, p, d, near("x", step), 4 + d)
        h_go(-step, p, None, core, 7 + d)

    def h_end(p):
        h_got(2, k, p, 0, 4)
        h_got(2, k, p, 1, 5)
        h_go(2, p, None, core, 9)

    h_missing = [1]

    def h_ready():
        if h_missing:
            h_missing.clear()
            for p in (0, 1):
                for n, step in enumerate((0, -1, 1, 2)):
                    h_got(step, 1 - k, p, None, 6 + n)

    def multiply_chips(u, chips):
        rows = pl.ds(*PARTS[u])

        def body(i, carry):
            n = sum(jnp.where(i == at, chip, 0) for at, chip in enumerate(chips))
            s = ((y + n // 4) % 4) * 4 + (z + n % 4) % 4
            acc[s // 8, rows, :] += jnp.dot(
                ps[s, 0, rows, :], hs[s % 8, pl.ds(0, T), :], preferred_element_type=F32
            ) + jnp.dot(ps[s, 1, rows, :], hs[s % 8, pl.ds(T, T), :], preferred_element_type=F32)
            return carry

        lax.fori_loop(0, len(chips), body, 0)

    def multiply(u, g):
        h_ready()
        if g == 1:
            p_end(u, 0)
        elif g == 3:
            p_end(u, 1)
            p_end(u, 2)
        elif g == 4:
            p_end(u, 3)
        multiply_chips(u, ((0, 1, 3, 4, 12), (2, 8), (5, 7, 13, 15), (9, 11, 6, 14), (10,))[g])

    def f_part(u, step, c, j=None):
        first = ((x + step + plane) % 4) * 4 + 2 * (1 - c)
        columns = pl.ds(*PARTS[u])
        return fs.at[pl.ds(first, 2), :, columns] if j is None else fs.at[first + j, :, columns]

    def f_go(u, step, j, device, index):
        ref = f_part(u, step, k, j)
        go(remote(ref, ref, f_send.at[10 * u + index], f_recv.at[10 * u + index], device))

    def f_got(u, step, c, j, index):
        got(f_part(u, step, c, j), f_recv.at[10 * u + index])

    def scatter(u):
        rows = pl.ds(*PARTS[u])
        for c in (0, 1):
            first = acc[c, rows, :] * qmask[c, rows, :].astype(F32)
            fb[c, rows, :] = first.astype(BF)
            ft[c, :, rows] = first.T.astype(BF)
            target = dev((y - x) % 4, 2 * k + xh, 2 * xl + c, 1 - zh)
            go(remote(ft.at[c, :, rows], fs.at[me, :, rows], f_send.at[10 * u + c], f_recv.at[10 * u + zl], target))

    def ring_start(u):
        for j in (0, 1):
            f_got(u, 0, k, j, j)
        f_go(u, 0, None, near("x", 1), 2)
        f_go(u, 0, None, near("x", -1), 3)
        f_go(u, 0, None, core, 6)

    def ring_pass(u, d):
        step = 1 - 2 * d
        f_got(u, -step, k, None, 2 + d)
        f_go(u, -step, d, near("x", step), 4 + d)
        f_go(u, -step, None, core, 7 + d)

    def ring_end(u):
        f_got(u, 2, k, 0, 4)
        f_got(u, 2, k, 1, 5)
        f_go(u, 2, None, core, 9)

    def multiply_second(u, r, places):
        rows, columns = pl.ds(256 * r, 256), pl.ds(*PARTS[u])

        def body(n, carry):
            step = sum(jnp.where(n == i, p[0], 0) for i, p in enumerate(places))
            c = sum(jnp.where(n == i, p[1], 0) for i, p in enumerate(places))
            sy = (x + step + plane) % 4
            for j in (0, 1):
                sz = 2 * (1 - c) + j
                for half in (0, 1):
                    sums[half, rows, columns] += jnp.dot(
                        ps[half * 8 + (sy % 2) * 4 + sz, sy // 2, rows, :], fs[sy * 4 + sz, :, columns],
                        preferred_element_type=F32,
                    )
            return carry

        lax.fori_loop(0, len(places), body, 0)

    def second(u, g, r):
        if g == 0:
            if r == 0:
                f_got(u, 0, 1 - k, None, 6)
            multiply_second(u, r, [(0, k), (-1, k), (1, k), (0, 1 - k)])
        else:
            if r == 0:
                f_got(u, -1, 1 - k, None, 7)
                f_got(u, 1, 1 - k, None, 8)
                f_got(u, 2, 1 - k, None, 9)
            multiply_second(u, r, [(2, k), (-1, 1 - k), (1, 1 - k), (2, 1 - k)])

    def columns_of(sy, sz, u):
        first = ((sy % 2) * 4 + sz) * 2 * T + (sy // 2) * T + PARTS[u][0]
        return pl.ds(pl.multiple_of(first, 128), PARTS[u][1])

    o_copy = []

    def finish(u):
        columns = pl.ds(*PARTS[u])
        for c in (0, 1):
            straight = fs[(2 * k + xh) * 4 + 2 * xl + c, :, columns].astype(F32)
            value = straight + fb[c, :, columns].astype(F32)
            gs[c, :, columns] = (value - sums[c, :, columns] * rmask[c, :, columns].astype(F32)).astype(BF)

        def rows_for(n):
            ty, tz = (y + n // 4) % 4, (z + n % 4) % 4
            b = (ty % 2) * 4 + tz
            return gs.at[ty // 2, pl.ds(pl.multiple_of(b * B, B), B), columns], dev(x, ty, tz, k)

        mine = out.at[:, columns_of(y, z, u)]
        local = pltpu.make_async_copy(rows_for(0)[0], mine, o_recv.at[16 * u + me])
        local.start()

        def copy(n):
            rows, device = rows_for(n)
            return remote(rows, mine, o_send.at[16 * u + n], o_recv.at[16 * u + me], device)

        def start(n, carry):
            copy(n).start()
            return carry

        lax.fori_loop(1, 16, start, 0)
        o_copy.append(copy)

    def masks():
        for n in (0, 1):
            got(qv.at[n], s_recv.at[n])
        got(rv.at[1 - yh], s_recv.at[2])
        eight = lax.broadcasted_iota(jnp.int32, (8, T), 0) == lax.broadcasted_iota(jnp.int32, (8, T), 1) // B
        narrow = spread(8 * yh)
        for c in (0, 1):
            qexp[...] = lax.dot_general(qv[c], eight.astype(F32), (((0,), (0,)), ((), ())), preferred_element_type=F32)
            q_wide = qexp[pl.ds(pl.multiple_of(k * 8, 8), 8), :]
            r_wide = 2.0 * jnp.dot(rv[c], narrow, preferred_element_type=F32)
            for i in range(8):
                qmask[c, pl.ds(i * B, B), :] = jnp.broadcast_to(q_wide[i : i + 1], (B, T)).astype(BF)
                rmask[c, pl.ds(i * B, B), :] = jnp.broadcast_to(r_wide[i : i + 1], (B, T)).astype(BF)

    own(0, 0)
    own(0, 1)
    rv[yh] = flags[3]
    q_copies = []
    for side in (0, 1):
        same = mirror & (k == side)
        copy = remote(
            flags.at[2], qv.at[zl], s_send.at[side], s_recv.at[zl],
            dev(2 * yl + zh, 2 * k + xh, 2 * xl + yh, side),
        )
        pl.when(jnp.logical_not(same))(copy.start)
        pl.when(same)(pltpu.make_async_copy(flags.at[2], qv.at[zl], s_recv.at[zl]).start)
        q_copies.append((same, copy))
    go(remote(rv.at[yh], rv.at[yh], s_send.at[2], s_recv.at[2], across))
    acc[...] = jnp.zeros_like(acc)
    sums[...] = jnp.zeros_like(sums)
    h_swap()
    turn(0, 0, 0); turn(0, 1, 0); h_start(0); pass_first(0, 1, 0); turn(0, 1, 1); pass_first(0, 1, 1)
    turn(0, 1, 2); pass_first(0, 0, 0); turn(0, 0, 1); pass_first(0, 0, 1); turn(0, 0, 2); pass_second(0, 0, 0, 0)
    pass_second(0, 0, 0, 1); turn(0, 1, 3); h_pass(0, 0); h_pass(0, 1); h_start(1); pass_second(0, 0, 1, 0)
    pass_second(0, 0, 1, 1); h_end(0); pass_second(0, 1, 0, 0); pass_second(0, 1, 0, 1); pass_second(0, 1, 1, 0)
    pass_second(0, 1, 1, 1); pass_second(0, 0, 2, 0); pass_second(0, 0, 2, 1); pass_second(0, 1, 2, 0)
    pass_second(0, 1, 2, 1); h_pass(1, 0); h_pass(1, 1); turn(0, 0, 3)
    masks()
    pass_second(0, 1, 3, 0); pass_second(0, 1, 3, 1); h_end(1)
    multiply(0, 0)
    own(1, 0); turn(1, 0, 0)
    multiply(0, 1)
    multiply(0, 2)
    pass_second(0, 0, 3, 0); pass_second(0, 0, 3, 1)
    multiply(0, 3)
    pass_second(1, 0, 0, 0); pass_second(1, 0, 0, 1); own(1, 1); turn(1, 1, 0); pass_first(1, 0, 0); turn(1, 0, 1)
    pass_first(1, 0, 1); turn(1, 0, 2)
    multiply(0, 4)
    scatter(0)
    turn(1, 0, 3); pass_second(1, 1, 0, 0); pass_second(1, 1, 0, 1); pass_first(1, 1, 0); turn(1, 1, 1)
    pass_first(1, 1, 1); turn(1, 1, 2)
    multiply(1, 0)
    pass_second(1, 0, 1, 0); pass_second(1, 0, 1, 1); pass_second(1, 0, 2, 0); pass_second(1, 0, 2, 1)
    pass_second(1, 1, 1, 0); pass_second(1, 1, 1, 1); own(2, 0); pass_second(1, 1, 2, 0); pass_second(1, 1, 2, 1)
    turn(2, 0, 0); ring_start(0); pass_second(1, 0, 3, 0); pass_second(1, 0, 3, 1); own(2, 1); turn(2, 1, 0)
    turn(1, 1, 3); pass_first(2, 0, 0); turn(2, 0, 1); pass_first(2, 0, 1); turn(2, 0, 2)
    multiply(1, 1)
    multiply(1, 2)
    pass_second(2, 1, 0, 0); pass_second(2, 1, 0, 1); pass_second(2, 0, 0, 0); pass_second(2, 0, 0, 1)
    pass_second(1, 1, 3, 0); pass_second(1, 1, 3, 1)
    multiply(1, 3)
    turn(2, 0, 3); pass_first(2, 1, 0); turn(2, 1, 1); pass_first(2, 1, 1); turn(2, 1, 2); ring_pass(0, 0)
    ring_pass(0, 1)
    multiply(2, 0)
    multiply(1, 4)
    scatter(1)
    pass_second(2, 0, 1, 0); pass_second(2, 0, 1, 1)
    second(0, 0, 0)
    pass_second(2, 1, 1, 0); pass_second(2, 1, 1, 1); pass_second(2, 0, 2, 0); pass_second(2, 0, 2, 1)
    pass_second(2, 1, 2, 0); pass_second(2, 1, 2, 1); ring_end(0); pass_second(2, 0, 3, 0); pass_second(2, 0, 3, 1)
    turn(2, 1, 3)
    multiply(2, 1)
    multiply(2, 2)
    second(0, 1, 0)
    pass_second(2, 1, 3, 0); pass_second(2, 1, 3, 1); ring_start(1)
    multiply(2, 3)
    multiply(2, 4)
    scatter(2)
    second(0, 0, 1)
    second(0, 1, 1)
    finish(0)
    ring_pass(1, 0); ring_pass(1, 1)
    second(1, 0, 0)
    ring_start(2)
    second(1, 0, 1)
    ring_end(1)
    second(1, 1, 0)
    second(1, 1, 1)
    finish(1)
    ring_pass(2, 0); ring_pass(2, 1)
    second(2, 0, 0)
    second(2, 0, 1)
    ring_end(2)
    second(2, 1, 0)
    second(2, 1, 1)
    finish(2)

    for u in range(N):
        def take(n, carry, u=u):
            got(out.at[:, columns_of(n // 4, n % 4, u)], o_recv.at[16 * u + n])
            return carry

        lax.fori_loop(0, 16, take, 0)
    for copy in pending:
        copy.wait_send()
    for same, copy in q_copies:
        pl.when(jnp.logical_not(same))(copy.wait_send)
    for copy in o_copy:
        def sent(n, carry, copy=copy):
            copy(n).wait_send()
            return carry

        lax.fori_loop(1, 16, sent, 0)


def per_device(hamiltonian, density, h_flags, p_flags, q_flags, r_flags):
    flags = jnp.stack([h_flags, p_flags, q_flags, r_flags]).astype(F32)
    flags = jnp.pad(flags, ((0, 0), (0, 0), (0, 112)))
    dma = pltpu.SemaphoreType.DMA
    rows = pl.pallas_call(
        kernel,
        out_shape=jax.ShapeDtypeStruct((64, 8192), BF),
        in_specs=[pl.BlockSpec(memory_space=pltpu.VMEM)] * 3,
        out_specs=pl.BlockSpec(memory_space=pl.ANY),
        scratch_shapes=[
            pltpu.VMEM((16, 2, T, T), BF),
            pltpu.VMEM((8, 2 * T, T), BF),
            pltpu.VMEM((16, T, T), BF),
            pltpu.VMEM((2, T, T), BF),
            pltpu.VMEM((2, T, T), F32),
            pltpu.VMEM((2, T, T), F32),
            pltpu.VMEM((2, T, T), BF),
            pltpu.VMEM((2, T, T), BF),
            pltpu.VMEM((2, T, T), BF),
            pltpu.VMEM((2, 8, 128), F32),
            pltpu.VMEM((2, 8, 128), F32),
            pltpu.VMEM((2, T, T), BF),
            pltpu.VMEM((2, T, T), BF),
            pltpu.VMEM((128, T), F32),
            dma((40 * N,)), dma((40 * N,)), dma((20,)), dma((20,)), dma((10 * N,)), dma((10 * N,)),
            dma((3,)), dma((3,)), dma((16 * N,)), dma((16 * N,)),
        ],
        compiler_params=pltpu.CompilerParams(
            collective_id=0, has_side_effects=True, vmem_limit_bytes=60 * 1024 * 1024
        ),
        cost_estimate=pl.CostEstimate(flops=2 * 2 * 512 * 8192 * 1024, bytes_accessed=4 << 20, transcendentals=0),
    )(hamiltonian, density, flags)
    return rows.astype(F32)


def solution(mesh):
    spec = P("row", "col")
    return jax.shard_map(
        per_device,
        mesh=mesh,
        in_specs=(spec,) * 6,
        out_specs=P(("row", "col"), None),
        check_vma=False,
    )
```

```python
import jax
import jax.numpy as jnp
from jax import lax
from jax.experimental import pallas as pl
from jax.experimental.pallas import tpu as pltpu
from jax.sharding import PartitionSpec as P

MESH = pl.DeviceIdType.MESH
BF = jnp.bfloat16
F32 = jnp.float32
B = 64
T = 512
PARTS = ((0, 256), (256, 128), (384, 128))
STREAMS = (((0, 160), (160, 96)), ((256, 64), (320, 64)), ((384, 64), (448, 64)))
N = len(PARTS)


def dev(x, y, z, k):
    return (x * 4 + (y // 2) * 2 + k, (y % 2) * 4 + z)


def kernel(
    ham, den, flags, out,
    ps, hs, fs, hm, acc, sums, fb, ft, gs, qv, rv, qmask, rmask, qexp,
    p_send, p_recv, h_send, h_recv, f_send, f_recv, s_send, s_recv, o_send, o_recv,
):
    row, col = lax.axis_index("row"), lax.axis_index("col")
    x, yh, k = row // 4, (row // 2) % 2, row % 2
    yl, z = col // 4, col % 4
    y = yh * 2 + yl
    zh, zl = z // 2, z % 2
    xh, xl = x // 2, x % 2
    me = y * 4 + z
    plane = 2 * yl + zh

    def near(axis, step):
        if axis == "x":
            return dev((x + step) % 4, y, z, k)
        if axis == "y":
            return dev(x, (y + step) % 4, z, k)
        return dev(x, y, (z + step) % 4, k)

    core = dev(x, y, z, 1 - k)
    across = near("y", 2)

    def remote(src, dst, send, recv, device):
        return pltpu.make_async_remote_copy(
            src_ref=src, dst_ref=dst, send_sem=send, recv_sem=recv,
            device_id=device, device_id_type=MESH,
        )

    barrier = pltpu.get_barrier_semaphore()

    def greet(device):
        pl.semaphore_signal(barrier, inc=1, device_id=device, device_id_type=MESH)

    def greet_plane(n, carry):
        greet(dev(x, (y + n // 4) % 4, (z + n % 4) % 4, k))
        return carry

    lax.fori_loop(1, 16, greet_plane, 0)
    greet(near("x", 1))
    greet(near("x", -1))
    greet(core)
    for j in (0, 1):
        greet(dev(plane, (x + plane + 2 * zl) % 4, 2 * ((1 - k + zl) % 2) + j, yh))
    mirror = (x == plane) & (y == 2 * k + xh) & (z == 2 * xl + yh)
    for c in (0, 1):
        pl.when(jnp.logical_not(mirror & (zl == c)))(
            lambda c=c: greet(dev(plane, 2 * zl + xh, 2 * xl + c, yh))
        )

    def spread(first):
        blocks = lax.broadcasted_iota(jnp.int32, (128, T), 0)
        places = lax.broadcasted_iota(jnp.int32, (128, T), 1) // B
        return (blocks == places + first).astype(F32)

    wides = [spread(8 * half) for half in (0, 1)]

    def masked(matrix, which, half, i):
        wide = jnp.dot(flags[which], wides[half], preferred_element_type=F32)
        return (matrix[pl.ds(i * B, B), pl.ds(half * T, T)].astype(F32) * wide[i : i + 1]).astype(BF)

    for half in (0, 1):
        for i in range(8):
            ps[me, half, pl.ds(i * B, B), :] = masked(den, 1, half, i)

    pl.semaphore_wait(barrier, 22 - mirror.astype(jnp.int32))

    pending = []

    def go(copy):
        copy.start()
        pending.append(copy)

    def got(dst, recv):
        remote(dst, dst, s_send.at[0], recv, core).wait_recv()

    AXES = (("y", "z"), ("z", "y"))
    OFFSET = (0, -1, 1, 2)

    def p_part(u, h, a, b, part):
        dy, dz = (a, b) if h == 0 else (b, a)
        s = ((y + dy) % 4) * 4 + (z + dz) % 4
        first, size = STREAMS[u][h]
        if part is not None:
            first, size = first + part * (size // 2), size // 2
        return ps.at[s, :, pl.ds(first, size), :]

    def p_go(u, h, a, b, part, axis, step, index):
        ref = p_part(u, h, a, b, part)
        go(remote(ref, ref, p_send.at[index], p_recv.at[index], near(axis, step)))

    def p_got(u, h, a, b, part, index):
        got(p_part(u, h, a, b, part), p_recv.at[index])

    def own(u, h):
        base = 40 * u + 20 * h
        p_go(u, h, 0, 0, None, AXES[h][0], 1, base)
        p_go(u, h, 0, 0, None, AXES[h][0], -1, base + 1)

    def pass_first(u, h, d):
        base, step = 40 * u + 20 * h, 1 - 2 * d
        p_got(u, h, -step, 0, None, base + d)
        p_go(u, h, -step, 0, d, AXES[h][0], step, base + 2 + d)

    def turn(u, h, j):
        base = 40 * u + 20 * h
        if j == 3:
            p_got(u, h, 2, 0, 0, base + 2)
            p_got(u, h, 2, 0, 1, base + 3)
        base += 4 + 4 * j
        p_go(u, h, OFFSET[j], 0, None, AXES[h][1], 1, base)
        p_go(u, h, OFFSET[j], 0, None, AXES[h][1], -1, base + 1)

    def pass_second(u, h, j, d):
        base, step = 40 * u + 20 * h + 4 + 4 * j, 1 - 2 * d
        p_got(u, h, OFFSET[j], -step, None, base + d)
        p_go(u, h, OFFSET[j], -step, d, AXES[h][1], step, base + 2 + d)

    def p_end(u, j):
        for h in (0, 1):
            base = 40 * u + 20 * h + 4 + 4 * j
            p_got(u, h, OFFSET[j], 2, 0, base + 2)
            p_got(u, h, OFFSET[j], 2, 1, base + 3)

    def h_part(step, c, p, part=None):
        first, size = (0, T) if part is None else (part * 256, 256)
        rows = pl.ds(pl.multiple_of(c * T + first, 256), size)
        return hs.at[((x + step) % 4) * 2 + (yh if p == 0 else 1 - yh), rows, :]

    def h_go(step, p, part, device, index):
        ref = h_part(step, k, p, part)
        go(remote(ref, ref, h_send.at[10 * p + index], h_recv.at[10 * p + index], device))

    def h_got(step, c, p, part, index):
        got(h_part(step, c, p, part), h_recv.at[10 * p + index])

    def h_swap():
        for half in (0, 1):
            for i in range(8):
                hm[half, pl.ds(i * B, B), :] = masked(ham, 0, half, i)
        go(remote(hm.at[1 - yh], h_part(0, k, 0), h_send.at[10], h_recv.at[10], across))
        h_local = pltpu.make_async_copy(hm.at[yh], h_part(0, k, 0), h_recv.at[0])
        h_local.start()
        h_local.wait()

    def h_start(p):
        if p == 1:
            h_got(0, k, 1, None, 0)
        h_go(0, p, None, near("x", 1), 2)
        h_go(0, p, None, near("x", -1), 3)
        h_go(0, p, None, core, 6)

    def h_pass(p, d):
        step = 1 - 2 * d
        h_got(-step, k, p, None, 2 + d)
        h_go(-step, p, d, near("x", step), 4 + d)
        h_go(-step, p, None, core, 7 + d)

    def h_end(p):
        h_got(2, k, p, 0, 4)
        h_got(2, k, p, 1, 5)
        h_go(2, p, None, core, 9)

    h_missing = [1]

    def h_ready():
        if h_missing:
            h_missing.clear()
            for p in (0, 1):
                for n, step in enumerate((0, -1, 1, 2)):
                    h_got(step, 1 - k, p, None, 6 + n)

    def pick(i, values):
        return sum(jnp.where(i == at, value, 0) for at, value in enumerate(values))

    def multiply_chips(u, chips):
        first, size = PARTS[u]
        rows = pl.ds(first, size)

        def body(i, carry):
            n = pick(i, chips)
            s = ((y + n // 4) % 2) * 4 + (z + n % 4) % 4
            left = jnp.concatenate(
                [jnp.concatenate([ps[s + 8 * c, half, rows, :] for half in (0, 1)], axis=1) for c in (0, 1)], axis=0
            )
            found = jnp.dot(left, hs[s], preferred_element_type=F32)
            for c in (0, 1):
                acc[c, rows, :] += found[c * size : (c + 1) * size]
            return carry

        lax.fori_loop(0, len(chips), body, 0)

    def multiply(u, g):
        h_ready()
        if g == 1:
            p_end(u, 0)
        elif g == 3:
            p_end(u, 1)
            p_end(u, 2)
        elif g == 4:
            p_end(u, 3)
        multiply_chips(u, ((4,), (0,), (5, 7), (1, 3, 6), (2,))[g])

    def f_part(u, step, c, j=None):
        first = ((x + step + plane + 2 * zl) % 4) * 4 + 2 * ((1 - c + zl) % 2)
        columns = pl.ds(*PARTS[u])
        return fs.at[pl.ds(first, 2), :, columns] if j is None else fs.at[first + j, :, columns]

    def f_go(u, step, j, device, index):
        ref = f_part(u, step, k, j)
        go(remote(ref, ref, f_send.at[10 * u + index], f_recv.at[10 * u + index], device))

    def f_got(u, step, c, j, index):
        got(f_part(u, step, c, j), f_recv.at[10 * u + index])

    def scatter(u):
        rows = pl.ds(*PARTS[u])
        for c in (0, 1):
            first = acc[c, rows, :] * qmask[c, rows, :].astype(F32)
            fb[c, rows, :] = first.astype(BF)
            ft[c, :, rows] = first.T.astype(BF)
            target = dev((y - x + 2 * c) % 4, 2 * k + xh, 2 * xl + c, (1 - zh + c) % 2)
            go(remote(ft.at[c, :, rows], fs.at[me, :, rows], f_send.at[10 * u + c], f_recv.at[10 * u + zl], target))

    def ring_start(u):
        for j in (0, 1):
            f_got(u, 0, k, j, j)
        f_go(u, 0, None, near("x", 1), 2)
        f_go(u, 0, None, near("x", -1), 3)
        f_go(u, 0, None, core, 6)

    def ring_pass(u, d):
        step = 1 - 2 * d
        f_got(u, -step, k, None, 2 + d)
        f_go(u, -step, d, near("x", step), 4 + d)
        f_go(u, -step, None, core, 7 + d)

    def ring_end(u):
        f_got(u, 2, k, 0, 4)
        f_got(u, 2, k, 1, 5)
        f_go(u, 2, None, core, 9)

    def multiply_second(v, which, places):
        rows, columns, size = pl.ds(*which), pl.ds(256 * v, 256), which[1]

        def body(n, carry):
            step = pick(n, [p[0] for p in places])
            c = pick(n, [p[1] for p in places])
            sy = (x + step + plane + 2 * zl) % 4
            sz = 2 * ((1 - c + zl) % 2)
            found = 0
            for j in (0, 1):
                s = (sy % 2) * 4 + sz + j
                left = jnp.concatenate([ps[s + 8 * half, sy // 2, rows, :] for half in (0, 1)], axis=0)
                found += jnp.dot(left, fs[sy * 4 + sz + j, :, columns], preferred_element_type=F32)
            for half in (0, 1):
                sums[half, rows, columns] += found[half * size : (half + 1) * size]
            return carry

        lax.fori_loop(0, len(places), body, 0)

    def second(v, g):
        if v == 0 and g < 2:
            if g == 0:
                f_got(0, 0, 1 - k, None, 6)
                multiply_second(0, (0, 256), [(0, k), (-1, k), (1, k), (0, 1 - k)])
            else:
                f_got(0, -1, 1 - k, None, 7)
                f_got(0, 1, 1 - k, None, 8)
                f_got(0, 2, 1 - k, None, 9)
                multiply_second(0, (0, 256), [(2, k), (-1, 1 - k), (1, 1 - k), (2, 1 - k)])
        elif v == 0:
            multiply_second(0, (256, 256), [(s, c) for s in OFFSET for c in (k, 1 - k)])
        elif g == 0:
            for u in range(1, N):
                f_got(u, 0, 1 - k, None, 6)
            multiply_second(1, (0, T), [(0, k), (-1, k), (1, k), (0, 1 - k)])
        else:
            for u in range(1, N):
                f_got(u, -1, 1 - k, None, 7)
                f_got(u, 1, 1 - k, None, 8)
                f_got(u, 2, 1 - k, None, 9)
            multiply_second(1, (0, T), [(2, k), (-1, 1 - k), (1, 1 - k), (2, 1 - k)])

    def columns_of(sy, sz, v):
        first = ((sy % 2) * 4 + sz) * 2 * T + (sy // 2) * T + 256 * v
        return pl.ds(pl.multiple_of(first, 256), 256)

    o_copy = []

    def finish(u):
        columns = pl.ds(256 * u, 256)
        for c in (0, 1):
            straight = fs[(2 * k + xh) * 4 + 2 * xl + c, :, columns].astype(F32)
            value = straight + fb[c, :, columns].astype(F32)
            gs[c, :, columns] = (value - sums[c, :, columns] * rmask[c, :, columns].astype(F32)).astype(BF)

        def rows_for(n):
            ty, tz = (y + n // 4) % 4, (z + n % 4) % 4
            b = (ty % 2) * 4 + tz
            return gs.at[ty // 2, pl.ds(pl.multiple_of(b * B, B), B), columns], dev(x, ty, tz, k)

        mine = out.at[:, columns_of(y, z, u)]
        local = pltpu.make_async_copy(rows_for(0)[0], mine, o_recv.at[16 * u + me])
        local.start()

        def copy(n):
            rows, device = rows_for(n)
            return remote(rows, mine, o_send.at[16 * u + n], o_recv.at[16 * u + me], device)

        def start(n, carry):
            copy(n).start()
            return carry

        lax.fori_loop(1, 16, start, 0)
        o_copy.append(copy)

    def masks():
        for n in (0, 1):
            got(qv.at[n], s_recv.at[n])
        got(rv.at[1 - yh], s_recv.at[2])
        eight = lax.broadcasted_iota(jnp.int32, (8, T), 0) == lax.broadcasted_iota(jnp.int32, (8, T), 1) // B
        narrow = spread(8 * yh)
        for c in (0, 1):
            qexp[...] = lax.dot_general(qv[c], eight.astype(F32), (((0,), (0,)), ((), ())), preferred_element_type=F32)
            q_wide = qexp[pl.ds(pl.multiple_of(k * 8, 8), 8), :]
            r_wide = 2.0 * jnp.dot(rv[c], narrow, preferred_element_type=F32)
            for i in range(8):
                qmask[c, pl.ds(i * B, B), :] = jnp.broadcast_to(q_wide[i : i + 1], (B, T)).astype(BF)
                rmask[c, pl.ds(i * B, B), :] = jnp.broadcast_to(r_wide[i : i + 1], (B, T)).astype(BF)

    own(0, 0)
    own(0, 1)
    rv[yh] = flags[3]
    q_copies = []
    for side in (0, 1):
        same = mirror & (k == side)
        copy = remote(
            flags.at[2], qv.at[zl], s_send.at[side], s_recv.at[zl],
            dev(2 * yl + zh, 2 * k + xh, 2 * xl + yh, side),
        )
        pl.when(jnp.logical_not(same))(copy.start)
        pl.when(same)(pltpu.make_async_copy(flags.at[2], qv.at[zl], s_recv.at[zl]).start)
        q_copies.append((same, copy))
    go(remote(rv.at[yh], rv.at[yh], s_send.at[2], s_recv.at[2], across))
    acc[...] = jnp.zeros_like(acc)
    sums[...] = jnp.zeros_like(sums)
    h_swap()
    turn(0, 0, 0); turn(0, 1, 0); h_start(0); pass_first(0, 1, 0); turn(0, 1, 1); pass_first(0, 1, 1)
    turn(0, 1, 2); pass_first(0, 0, 0); turn(0, 0, 1); pass_first(0, 0, 1); turn(0, 0, 2); pass_second(0, 0, 0, 0)
    pass_second(0, 0, 0, 1); turn(0, 1, 3); h_pass(0, 0); h_pass(0, 1); h_start(1); pass_second(0, 0, 1, 0)
    pass_second(0, 0, 1, 1); h_end(0); pass_second(0, 1, 0, 0); pass_second(0, 1, 0, 1); pass_second(0, 1, 1, 0)
    pass_second(0, 1, 1, 1); pass_second(0, 0, 2, 0); pass_second(0, 0, 2, 1); pass_second(0, 1, 2, 0)
    pass_second(0, 1, 2, 1); h_pass(1, 0); h_pass(1, 1); turn(0, 0, 3)
    masks()
    pass_second(0, 1, 3, 0); pass_second(0, 1, 3, 1); h_end(1)
    multiply(0, 0)
    own(1, 0); turn(1, 0, 0)
    multiply(0, 1)
    multiply(0, 2)
    pass_second(0, 0, 3, 0); pass_second(0, 0, 3, 1)
    multiply(0, 3)
    pass_second(1, 0, 0, 0); pass_second(1, 0, 0, 1); own(1, 1); turn(1, 1, 0); pass_first(1, 0, 0); turn(1, 0, 1)
    pass_first(1, 0, 1); turn(1, 0, 2)
    multiply(0, 4)
    scatter(0)
    turn(1, 0, 3); pass_second(1, 1, 0, 0); pass_second(1, 1, 0, 1); pass_first(1, 1, 0); turn(1, 1, 1)
    pass_first(1, 1, 1); turn(1, 1, 2)
    multiply(1, 0)
    pass_second(1, 0, 1, 0); pass_second(1, 0, 1, 1); pass_second(1, 0, 2, 0); pass_second(1, 0, 2, 1)
    pass_second(1, 1, 1, 0); pass_second(1, 1, 1, 1); own(2, 0); pass_second(1, 1, 2, 0); pass_second(1, 1, 2, 1)
    turn(2, 0, 0); ring_start(0); pass_second(1, 0, 3, 0); pass_second(1, 0, 3, 1); turn(1, 1, 3)
    multiply(1, 1)
    pass_first(2, 0, 0); turn(2, 0, 1); pass_first(2, 0, 1); turn(2, 0, 2)
    multiply(1, 2)
    own(2, 1); turn(2, 1, 0); pass_second(1, 1, 3, 0); pass_second(1, 1, 3, 1)
    multiply(1, 3)
    turn(2, 0, 3); pass_second(2, 0, 0, 0); pass_second(2, 0, 0, 1); pass_second(2, 1, 0, 0)
    pass_second(2, 1, 0, 1); pass_second(2, 0, 1, 0); pass_second(2, 0, 1, 1); ring_pass(0, 0); ring_pass(0, 1)
    multiply(1, 4)
    scatter(1)
    pass_second(2, 0, 2, 0); pass_second(2, 0, 2, 1)
    second(0, 0)
    pass_first(2, 1, 0); turn(2, 1, 1); pass_first(2, 1, 1); turn(2, 1, 2)
    multiply(2, 0)
    ring_end(0); pass_second(2, 0, 3, 0); pass_second(2, 0, 3, 1); pass_second(2, 1, 1, 0); pass_second(2, 1, 1, 1)
    second(0, 1)
    pass_second(2, 1, 2, 0); pass_second(2, 1, 2, 1); ring_start(1); turn(2, 1, 3)
    multiply(2, 1)
    multiply(2, 2)
    pass_second(2, 1, 3, 0); pass_second(2, 1, 3, 1)
    multiply(2, 3)
    ring_pass(1, 0); ring_pass(1, 1)
    multiply(2, 4)
    scatter(2)
    second(0, 2)
    ring_end(1)
    finish(0)
    ring_start(2); ring_pass(2, 0); ring_pass(2, 1)
    second(1, 0)
    ring_end(2)
    second(1, 1)
    finish(1)

    for u in (0, 1):
        def take(n, carry, u=u):
            got(out.at[:, columns_of(n // 4, n % 4, u)], o_recv.at[16 * u + n])
            return carry

        lax.fori_loop(0, 16, take, 0)
    for copy in pending:
        copy.wait_send()
    for same, copy in q_copies:
        pl.when(jnp.logical_not(same))(copy.wait_send)
    for copy in o_copy:
        def sent(n, carry, copy=copy):
            copy(n).wait_send()
            return carry

        lax.fori_loop(1, 16, sent, 0)


def per_device(hamiltonian, density, h_flags, p_flags, q_flags, r_flags):
    flags = jnp.stack([h_flags, p_flags, q_flags, r_flags]).astype(F32)
    flags = jnp.pad(flags, ((0, 0), (0, 0), (0, 112)))
    dma = pltpu.SemaphoreType.DMA
    rows = pl.pallas_call(
        kernel,
        out_shape=jax.ShapeDtypeStruct((64, 8192), BF),
        in_specs=[pl.BlockSpec(memory_space=pltpu.VMEM)] * 3,
        out_specs=pl.BlockSpec(memory_space=pl.ANY),
        scratch_shapes=[
            pltpu.VMEM((16, 2, T, T), BF),
            pltpu.VMEM((8, 2 * T, T), BF),
            pltpu.VMEM((16, T, T), BF),
            pltpu.VMEM((2, T, T), BF),
            pltpu.VMEM((2, T, T), F32),
            pltpu.VMEM((2, T, T), F32),
            pltpu.VMEM((2, T, T), BF),
            pltpu.VMEM((2, T, T), BF),
            pltpu.VMEM((2, T, T), BF),
            pltpu.VMEM((2, 8, 128), F32),
            pltpu.VMEM((2, 8, 128), F32),
            pltpu.VMEM((2, T, T), BF),
            pltpu.VMEM((2, T, T), BF),
            pltpu.VMEM((128, T), F32),
            dma((40 * N,)), dma((40 * N,)), dma((20,)), dma((20,)), dma((10 * N,)), dma((10 * N,)),
            dma((3,)), dma((3,)), dma((32,)), dma((32,)),
        ],
        compiler_params=pltpu.CompilerParams(
            collective_id=0, has_side_effects=True, vmem_limit_bytes=60 * 1024 * 1024
        ),
        cost_estimate=pl.CostEstimate(flops=2 * 2 * 512 * 8192 * 1024, bytes_accessed=4 << 20, transcendentals=0),
    )(hamiltonian, density, flags)
    return rows.astype(F32)


def solution(mesh):
    spec = P("row", "col")
    return jax.shard_map(
        per_device,
        mesh=mesh,
        in_specs=(spec,) * 6,
        out_specs=P(("row", "col"), None),
        check_vma=False,
    )
```

```python
import jax
import jax.numpy as jnp
from jax import lax
from jax.experimental import pallas as pl
from jax.experimental.pallas import tpu as pltpu
from jax.sharding import PartitionSpec as P

MESH = pl.DeviceIdType.MESH
BF = jnp.bfloat16
F32 = jnp.float32
B = 64
T = 512
PARTS = ((0, 256), (256, 128), (384, 128))
STREAMS = (((0, 144), (144, 112)), ((256, 64), (320, 64)), ((384, 64), (448, 64)))
N = len(PARTS)


def dev(x, y, z, k):
    return (x * 4 + (y // 2) * 2 + k, (y % 2) * 4 + z)


def kernel(
    ham, den, flags, out,
    ps, hs, fs, hm, acc, sums, fb, ft, gs, qv, rv, qmask, rmask, qexp,
    p_send, p_recv, h_send, h_recv, f_send, f_recv, s_send, s_recv, o_send, o_recv,
):
    row, col = lax.axis_index("row"), lax.axis_index("col")
    x, yh, k = row // 4, (row // 2) % 2, row % 2
    yl, z = col // 4, col % 4
    y = yh * 2 + yl
    zh, zl = z // 2, z % 2
    xh, xl = x // 2, x % 2
    me = y * 4 + z
    plane = 2 * yl + zh

    def near(axis, step):
        if axis == "x":
            return dev((x + step) % 4, y, z, k)
        if axis == "y":
            return dev(x, (y + step) % 4, z, k)
        return dev(x, y, (z + step) % 4, k)

    core = dev(x, y, z, 1 - k)
    across = near("y", 2)

    def remote(src, dst, send, recv, device):
        return pltpu.make_async_remote_copy(
            src_ref=src, dst_ref=dst, send_sem=send, recv_sem=recv,
            device_id=device, device_id_type=MESH,
        )

    barrier = pltpu.get_barrier_semaphore()

    def greet(device):
        pl.semaphore_signal(barrier, inc=1, device_id=device, device_id_type=MESH)

    def greet_plane(n, carry):
        greet(dev(x, (y + n // 4) % 4, (z + n % 4) % 4, k))
        return carry

    lax.fori_loop(1, 16, greet_plane, 0)
    greet(near("x", 1))
    greet(near("x", -1))
    greet(core)
    for j in (0, 1):
        greet(dev(plane, (x + plane + 2 * zl) % 4, 2 * ((1 - k + zl) % 2) + j, yh))
    mirror = (x == plane) & (y == 2 * k + xh) & (z == 2 * xl + yh)
    for c in (0, 1):
        pl.when(jnp.logical_not(mirror & (zl == c)))(
            lambda c=c: greet(dev(plane, 2 * zl + xh, 2 * xl + c, yh))
        )

    def spread(first):
        blocks = lax.broadcasted_iota(jnp.int32, (128, T), 0)
        places = lax.broadcasted_iota(jnp.int32, (128, T), 1) // B
        return (blocks == places + first).astype(F32)

    wides = [spread(8 * half) for half in (0, 1)]

    def masked(matrix, which, half, i):
        wide = jnp.dot(flags[which], wides[half], preferred_element_type=F32)
        return (matrix[pl.ds(i * B, B), pl.ds(half * T, T)].astype(F32) * wide[i : i + 1]).astype(BF)

    for half in (0, 1):
        for i in range(8):
            ps[me, half, pl.ds(i * B, B), :] = masked(den, 1, half, i)

    pl.semaphore_wait(barrier, 22 - mirror.astype(jnp.int32))

    pending = []

    def go(copy):
        copy.start()
        pending.append(copy)

    def got(dst, recv):
        remote(dst, dst, s_send.at[0], recv, core).wait_recv()

    AXES = (("y", "z"), ("z", "y"))
    OFFSET = (0, -1, 1, 2)

    def p_part(u, h, a, b, part):
        dy, dz = (a, b) if h == 0 else (b, a)
        s = ((y + dy) % 4) * 4 + (z + dz) % 4
        first, size = STREAMS[u][h]
        if part is not None:
            cut = (size // 2 + 15) // 16 * 16
            first, size = (first, cut) if part == 0 else (first + cut, size - cut)
        return ps.at[s, :, pl.ds(first, size), :]

    def p_go(u, h, a, b, part, axis, step, index):
        ref = p_part(u, h, a, b, part)
        go(remote(ref, ref, p_send.at[index], p_recv.at[index], near(axis, step)))

    def p_got(u, h, a, b, part, index):
        got(p_part(u, h, a, b, part), p_recv.at[index])

    def own(u, h):
        base = 40 * u + 20 * h
        p_go(u, h, 0, 0, None, AXES[h][0], 1, base)
        p_go(u, h, 0, 0, None, AXES[h][0], -1, base + 1)

    def pass_first(u, h, d):
        base, step = 40 * u + 20 * h, 1 - 2 * d
        p_got(u, h, -step, 0, None, base + d)
        p_go(u, h, -step, 0, d, AXES[h][0], step, base + 2 + d)

    def turn(u, h, j):
        base = 40 * u + 20 * h
        if j == 3:
            p_got(u, h, 2, 0, 0, base + 2)
            p_got(u, h, 2, 0, 1, base + 3)
        base += 4 + 4 * j
        p_go(u, h, OFFSET[j], 0, None, AXES[h][1], 1, base)
        p_go(u, h, OFFSET[j], 0, None, AXES[h][1], -1, base + 1)

    def pass_second(u, h, j, d):
        base, step = 40 * u + 20 * h + 4 + 4 * j, 1 - 2 * d
        p_got(u, h, OFFSET[j], -step, None, base + d)
        p_go(u, h, OFFSET[j], -step, d, AXES[h][1], step, base + 2 + d)

    def p_end(u, j):
        for h in (0, 1):
            base = 40 * u + 20 * h + 4 + 4 * j
            p_got(u, h, OFFSET[j], 2, 0, base + 2)
            p_got(u, h, OFFSET[j], 2, 1, base + 3)

    def h_part(step, c, p, part=None):
        first, size = (0, T) if part is None else (part * 256, 256)
        rows = pl.ds(pl.multiple_of(c * T + first, 256), size)
        return hs.at[((x + step) % 4) * 2 + (yh if p == 0 else 1 - yh), rows, :]

    def h_go(step, p, part, device, index):
        ref = h_part(step, k, p, part)
        go(remote(ref, ref, h_send.at[10 * p + index], h_recv.at[10 * p + index], device))

    def h_got(step, c, p, part, index):
        got(h_part(step, c, p, part), h_recv.at[10 * p + index])

    def h_swap():
        for half in (0, 1):
            for i in range(8):
                hm[half, pl.ds(i * B, B), :] = masked(ham, 0, half, i)
        go(remote(hm.at[1 - yh], h_part(0, k, 0), h_send.at[10], h_recv.at[10], across))
        h_local = pltpu.make_async_copy(hm.at[yh], h_part(0, k, 0), h_recv.at[0])
        h_local.start()
        h_local.wait()

    def h_start(p):
        if p == 1:
            h_got(0, k, 1, None, 0)
        h_go(0, p, None, near("x", 1), 2)
        h_go(0, p, None, near("x", -1), 3)
        h_go(0, p, None, core, 6)

    def h_pass(p, d):
        step = 1 - 2 * d
        h_got(-step, k, p, None, 2 + d)
        h_go(-step, p, d, near("x", step), 4 + d)
        h_go(-step, p, None, core, 7 + d)

    def h_end(p):
        h_got(2, k, p, 0, 4)
        h_got(2, k, p, 1, 5)
        h_go(2, p, None, core, 9)

    h_missing = [1]

    def h_ready():
        if h_missing:
            h_missing.clear()
            for p in (0, 1):
                for n, step in enumerate((0, -1, 1, 2)):
                    h_got(step, 1 - k, p, None, 6 + n)

    def pick(i, values):
        return sum(jnp.where(i == at, value, 0) for at, value in enumerate(values))

    def multiply_chips(u, chips):
        first, size = PARTS[u]
        rows = pl.ds(first, size)

        def body(i, carry):
            n = pick(i, chips)
            s = ((y + n // 4) % 2) * 4 + (z + n % 4) % 4
            left = jnp.concatenate(
                [jnp.concatenate([ps[s + 8 * c, half, rows, :] for half in (0, 1)], axis=1) for c in (0, 1)], axis=0
            )
            found = jnp.dot(left, hs[s], preferred_element_type=F32)
            for c in (0, 1):
                acc[c, rows, :] += found[c * size : (c + 1) * size]
            return carry

        lax.fori_loop(0, len(chips), body, 0)

    def multiply(u, g):
        h_ready()
        if g == 1:
            p_end(u, 0)
        elif g == 3:
            p_end(u, 1)
            p_end(u, 2)
        elif g == 4:
            p_end(u, 3)
        multiply_chips(u, ((4,), (0,), (5, 7), (1, 3, 6), (2,))[g])

    def f_part(u, step, c, j=None):
        first = ((x + step + plane + 2 * zl) % 4) * 4 + 2 * ((1 - c + zl) % 2)
        columns = pl.ds(*PARTS[u])
        return fs.at[pl.ds(first, 2), :, columns] if j is None else fs.at[first + j, :, columns]

    def f_go(u, step, j, device, index):
        ref = f_part(u, step, k, j)
        go(remote(ref, ref, f_send.at[10 * u + index], f_recv.at[10 * u + index], device))

    def f_got(u, step, c, j, index):
        got(f_part(u, step, c, j), f_recv.at[10 * u + index])

    def scatter(u):
        rows = pl.ds(*PARTS[u])
        for c in (0, 1):
            first = acc[c, rows, :] * qmask[c, rows, :].astype(F32)
            fb[c, rows, :] = first.astype(BF)
            ft[c, :, rows] = first.T.astype(BF)
            target = dev((y - x + 2 * c) % 4, 2 * k + xh, 2 * xl + c, (1 - zh + c) % 2)
            go(remote(ft.at[c, :, rows], fs.at[me, :, rows], f_send.at[10 * u + c], f_recv.at[10 * u + zl], target))

    def ring_start(u):
        for j in (0, 1):
            f_got(u, 0, k, j, j)
        f_go(u, 0, None, near("x", 1), 2)
        f_go(u, 0, None, near("x", -1), 3)
        f_go(u, 0, None, core, 6)

    def ring_pass(u, d):
        step = 1 - 2 * d
        f_got(u, -step, k, None, 2 + d)
        f_go(u, -step, d, near("x", step), 4 + d)
        f_go(u, -step, None, core, 7 + d)

    def ring_end(u):
        f_got(u, 2, k, 0, 4)
        f_got(u, 2, k, 1, 5)
        f_go(u, 2, None, core, 9)

    def multiply_second(v, which, places):
        rows, columns, size = pl.ds(*which), pl.ds(256 * v, 256), which[1]

        def body(n, carry):
            step = pick(n, [p[0] for p in places])
            c = pick(n, [p[1] for p in places])
            sy = (x + step + plane + 2 * zl) % 4
            sz = 2 * ((1 - c + zl) % 2)
            found = 0
            for j in (0, 1):
                s = (sy % 2) * 4 + sz + j
                left = jnp.concatenate([ps[s + 8 * half, sy // 2, rows, :] for half in (0, 1)], axis=0)
                found += jnp.dot(left, fs[sy * 4 + sz + j, :, columns], preferred_element_type=F32)
            for half in (0, 1):
                sums[half, rows, columns] += found[half * size : (half + 1) * size]
            return carry

        lax.fori_loop(0, len(places), body, 0)

    def second(v, g):
        if v == 0 and g < 2:
            if g == 0:
                f_got(0, 0, 1 - k, None, 6)
                multiply_second(0, (0, 256), [(0, k), (-1, k), (1, k), (0, 1 - k)])
            else:
                f_got(0, -1, 1 - k, None, 7)
                f_got(0, 1, 1 - k, None, 8)
                f_got(0, 2, 1 - k, None, 9)
                multiply_second(0, (0, 256), [(2, k), (-1, 1 - k), (1, 1 - k), (2, 1 - k)])
        elif v == 0:
            multiply_second(0, (256, 256), [(s, c) for s in OFFSET for c in (k, 1 - k)])
        elif g == 0:
            for u in range(1, N):
                f_got(u, 0, 1 - k, None, 6)
            multiply_second(1, (0, T), [(0, k), (-1, k), (1, k), (0, 1 - k)])
        else:
            for u in range(1, N):
                f_got(u, -1, 1 - k, None, 7)
                f_got(u, 1, 1 - k, None, 8)
                f_got(u, 2, 1 - k, None, 9)
            multiply_second(1, (0, T), [(2, k), (-1, 1 - k), (1, 1 - k), (2, 1 - k)])

    def columns_of(sy, sz, v):
        first = ((sy % 2) * 4 + sz) * 2 * T + (sy // 2) * T + 256 * v
        return pl.ds(pl.multiple_of(first, 256), 256)

    o_copy = []

    def finish(u):
        columns = pl.ds(256 * u, 256)
        for c in (0, 1):
            straight = fs[(2 * k + xh) * 4 + 2 * xl + c, :, columns].astype(F32)
            value = straight + fb[c, :, columns].astype(F32)
            gs[c, :, columns] = (value - sums[c, :, columns] * rmask[c, :, columns].astype(F32)).astype(BF)

        def rows_for(n):
            ty, tz = (y + n // 4) % 4, (z + n % 4) % 4
            b = (ty % 2) * 4 + tz
            return gs.at[ty // 2, pl.ds(pl.multiple_of(b * B, B), B), columns], dev(x, ty, tz, k)

        mine = out.at[:, columns_of(y, z, u)]
        local = pltpu.make_async_copy(rows_for(0)[0], mine, o_recv.at[16 * u + me])
        local.start()

        def copy(n):
            rows, device = rows_for(n)
            return remote(rows, mine, o_send.at[16 * u + n], o_recv.at[16 * u + me], device)

        def start(n, carry):
            copy(n).start()
            return carry

        lax.fori_loop(1, 16, start, 0)
        o_copy.append(copy)

    def masks():
        for n in (0, 1):
            got(qv.at[n], s_recv.at[n])
        got(rv.at[1 - yh], s_recv.at[2])
        eight = lax.broadcasted_iota(jnp.int32, (8, T), 0) == lax.broadcasted_iota(jnp.int32, (8, T), 1) // B
        narrow = spread(8 * yh)
        for c in (0, 1):
            qexp[...] = lax.dot_general(qv[c], eight.astype(F32), (((0,), (0,)), ((), ())), preferred_element_type=F32)
            q_wide = qexp[pl.ds(pl.multiple_of(k * 8, 8), 8), :]
            r_wide = 2.0 * jnp.dot(rv[c], narrow, preferred_element_type=F32)
            for i in range(8):
                qmask[c, pl.ds(i * B, B), :] = jnp.broadcast_to(q_wide[i : i + 1], (B, T)).astype(BF)
                rmask[c, pl.ds(i * B, B), :] = jnp.broadcast_to(r_wide[i : i + 1], (B, T)).astype(BF)

    own(0, 0); own(0, 1)
    rv[yh] = flags[3]
    q_copies = []
    for side in (0, 1):
        same = mirror & (k == side)
        copy = remote(
            flags.at[2], qv.at[zl], s_send.at[side], s_recv.at[zl],
            dev(2 * yl + zh, 2 * k + xh, 2 * xl + yh, side),
        )
        pl.when(jnp.logical_not(same))(copy.start)
        pl.when(same)(pltpu.make_async_copy(flags.at[2], qv.at[zl], s_recv.at[zl]).start)
        q_copies.append((same, copy))
    go(remote(rv.at[yh], rv.at[yh], s_send.at[2], s_recv.at[2], across))
    acc[...] = jnp.zeros_like(acc)
    sums[...] = jnp.zeros_like(sums)
    h_swap()
    h_start(0); turn(0, 1, 0); turn(0, 0, 0); pass_first(0, 1, 0); turn(0, 1, 1); pass_first(0, 1, 1)
    turn(0, 1, 2); pass_first(0, 0, 0); turn(0, 0, 1); pass_first(0, 0, 1); turn(0, 0, 2); pass_second(0, 0, 0, 0)
    pass_second(0, 0, 0, 1); h_pass(0, 0); h_pass(0, 1); turn(0, 1, 3); h_start(1); pass_second(0, 0, 1, 0)
    pass_second(0, 0, 1, 1); h_end(0); pass_second(0, 1, 0, 0); pass_second(0, 1, 0, 1); pass_second(0, 0, 2, 0)
    pass_second(0, 0, 2, 1); pass_second(0, 1, 1, 0); pass_second(0, 1, 1, 1); pass_second(0, 1, 2, 0)
    pass_second(0, 1, 2, 1); h_pass(1, 0); own(1, 0); turn(1, 0, 0); h_pass(1, 1); turn(0, 0, 3)
    masks()
    pass_second(1, 0, 0, 0); pass_second(1, 0, 0, 1); pass_second(0, 1, 3, 0); pass_second(0, 1, 3, 1); h_end(1)
    own(1, 1); turn(1, 1, 0); pass_second(0, 0, 3, 0); pass_second(0, 0, 3, 1)
    multiply(0, 0)
    multiply(0, 1)
    multiply(0, 2)
    pass_first(1, 1, 0); turn(1, 1, 1); pass_first(1, 1, 1); turn(1, 1, 2); pass_first(1, 0, 0); turn(1, 0, 1)
    pass_first(1, 0, 1); turn(1, 0, 2)
    multiply(0, 3)
    multiply(0, 4)
    scatter(0)
    turn(1, 1, 3); pass_second(1, 1, 0, 0); pass_second(1, 1, 0, 1)
    multiply(1, 0)
    pass_second(1, 0, 1, 0); pass_second(1, 0, 1, 1); pass_second(1, 1, 1, 0); pass_second(1, 1, 1, 1)
    pass_second(1, 0, 2, 0); pass_second(1, 0, 2, 1); pass_second(1, 1, 2, 0); pass_second(1, 1, 2, 1)
    turn(1, 0, 3); own(2, 0); turn(2, 0, 0); ring_start(0); own(2, 1); pass_second(1, 0, 3, 0)
    pass_second(1, 1, 3, 0); pass_second(1, 1, 3, 1); pass_second(1, 0, 3, 1); turn(2, 1, 0)
    multiply(1, 1)
    multiply(1, 2)
    pass_second(2, 0, 0, 0); pass_second(2, 0, 0, 1)
    multiply(1, 3)
    pass_first(2, 1, 0); turn(2, 1, 1); pass_first(2, 1, 1); turn(2, 1, 2); pass_first(2, 0, 0); turn(2, 0, 1)
    pass_first(2, 0, 1); turn(2, 0, 2)
    multiply(1, 4)
    scatter(1)
    turn(2, 1, 3); pass_second(2, 1, 0, 0); pass_second(2, 1, 0, 1)
    multiply(2, 0)
    pass_second(2, 0, 1, 0); ring_pass(0, 0); ring_pass(0, 1); pass_second(2, 0, 1, 1)
    second(0, 0)
    pass_second(2, 1, 1, 0); pass_second(2, 1, 1, 1); pass_second(2, 0, 2, 0); pass_second(2, 0, 2, 1)
    pass_second(2, 1, 2, 0); pass_second(2, 1, 2, 1); turn(2, 0, 3); ring_end(0); ring_start(1)
    pass_second(2, 1, 3, 0); pass_second(2, 1, 3, 1); pass_second(2, 0, 3, 0); pass_second(2, 0, 3, 1)
    multiply(2, 1)
    multiply(2, 2)
    second(0, 1)
    multiply(2, 3)
    multiply(2, 4)
    scatter(2)
    second(0, 2)
    ring_pass(1, 0); ring_pass(1, 1)
    finish(0)
    ring_start(2); ring_end(1); ring_pass(2, 0); ring_pass(2, 1)
    second(1, 0)
    ring_end(2)
    second(1, 1)
    finish(1)

    for u in (0, 1):
        def take(n, carry, u=u):
            got(out.at[:, columns_of(n // 4, n % 4, u)], o_recv.at[16 * u + n])
            return carry

        lax.fori_loop(0, 16, take, 0)
    for copy in pending:
        copy.wait_send()
    for same, copy in q_copies:
        pl.when(jnp.logical_not(same))(copy.wait_send)
    for copy in o_copy:
        def sent(n, carry, copy=copy):
            copy(n).wait_send()
            return carry

        lax.fori_loop(1, 16, sent, 0)


def per_device(hamiltonian, density, h_flags, p_flags, q_flags, r_flags):
    flags = jnp.stack([h_flags, p_flags, q_flags, r_flags]).astype(F32)
    flags = jnp.pad(flags, ((0, 0), (0, 0), (0, 112)))
    dma = pltpu.SemaphoreType.DMA
    rows = pl.pallas_call(
        kernel,
        out_shape=jax.ShapeDtypeStruct((64, 8192), BF),
        in_specs=[pl.BlockSpec(memory_space=pltpu.VMEM)] * 3,
        out_specs=pl.BlockSpec(memory_space=pl.ANY),
        scratch_shapes=[
            pltpu.VMEM((16, 2, T, T), BF),
            pltpu.VMEM((8, 2 * T, T), BF),
            pltpu.VMEM((16, T, T), BF),
            pltpu.VMEM((2, T, T), BF),
            pltpu.VMEM((2, T, T), F32),
            pltpu.VMEM((2, T, T), F32),
            pltpu.VMEM((2, T, T), BF),
            pltpu.VMEM((2, T, T), BF),
            pltpu.VMEM((2, T, T), BF),
            pltpu.VMEM((2, 8, 128), F32),
            pltpu.VMEM((2, 8, 128), F32),
            pltpu.VMEM((2, T, T), BF),
            pltpu.VMEM((2, T, T), BF),
            pltpu.VMEM((128, T), F32),
            dma((40 * N,)), dma((40 * N,)), dma((20,)), dma((20,)), dma((10 * N,)), dma((10 * N,)),
            dma((3,)), dma((3,)), dma((32,)), dma((32,)),
        ],
        compiler_params=pltpu.CompilerParams(
            collective_id=0, has_side_effects=True, vmem_limit_bytes=60 * 1024 * 1024
        ),
        cost_estimate=pl.CostEstimate(flops=2 * 2 * 512 * 8192 * 1024, bytes_accessed=4 << 20, transcendentals=0),
    )(hamiltonian, density, flags)
    return rows.astype(F32)


def solution(mesh):
    spec = P("row", "col")
    return jax.shard_map(
        per_device,
        mesh=mesh,
        in_specs=(spec,) * 6,
        out_specs=P(("row", "col"), None),
        check_vma=False,
    )
```

```python
import jax
import jax.numpy as jnp
from jax import lax
from jax.experimental import pallas as pl
from jax.experimental.pallas import tpu as pltpu
from jax.sharding import PartitionSpec as P

MESH = pl.DeviceIdType.MESH
BF = jnp.bfloat16
F32 = jnp.float32
B = 64
T = 512
PARTS = ((0, 256), (256, 128), (384, 128))
STREAMS = (((0, 144), (144, 112)), ((256, 64), (320, 64)), ((384, 64), (448, 64)))
N = len(PARTS)


def dev(x, y, z, k):
    return (x * 4 + (y // 2) * 2 + k, (y % 2) * 4 + z)


def kernel(
    ham, den, h_flags, p_flags, q_flags, r_flags, out,
    flags, ps, hs, fs, hm, acc, sums, fb, ft, gs, qv, rv, qmask, rmask, qexp,
    p_send, p_recv, h_send, h_recv, f_send, f_recv, s_send, s_recv, o_send, o_recv,
):
    row, col = lax.axis_index("row"), lax.axis_index("col")
    x, yh, k = row // 4, (row // 2) % 2, row % 2
    yl, z = col // 4, col % 4
    y = yh * 2 + yl
    zh, zl = z // 2, z % 2
    xh, xl = x // 2, x % 2
    me = y * 4 + z
    plane = 2 * yl + zh

    def near(axis, step):
        if axis == "x":
            return dev((x + step) % 4, y, z, k)
        if axis == "y":
            return dev(x, (y + step) % 4, z, k)
        return dev(x, y, (z + step) % 4, k)

    core = dev(x, y, z, 1 - k)
    across = near("y", 2)

    def remote(src, dst, send, recv, device):
        return pltpu.make_async_remote_copy(
            src_ref=src, dst_ref=dst, send_sem=send, recv_sem=recv,
            device_id=device, device_id_type=MESH,
        )

    barrier = pltpu.get_barrier_semaphore()

    def greet(device):
        pl.semaphore_signal(barrier, inc=1, device_id=device, device_id_type=MESH)

    def greet_plane(n, carry):
        greet(dev(x, (y + n // 4) % 4, (z + n % 4) % 4, k))
        return carry

    lax.fori_loop(1, 16, greet_plane, 0)
    greet(near("x", 1))
    greet(near("x", -1))
    greet(core)
    for j in (0, 1):
        greet(dev(plane, (x + plane + 2 * zl) % 4, 2 * ((1 - k + zl) % 2) + j, yh))
    mirror = (x == plane) & (y == 2 * k + xh) & (z == 2 * xl + yh)
    for c in (0, 1):
        pl.when(jnp.logical_not(mirror & (zl == c)))(
            lambda c=c: greet(dev(plane, 2 * zl + xh, 2 * xl + c, yh))
        )

    def spread(first):
        blocks = lax.broadcasted_iota(jnp.int32, (128, T), 0)
        places = lax.broadcasted_iota(jnp.int32, (128, T), 1) // B
        return (blocks == places + first).astype(F32)

    flags[...] = jnp.zeros_like(flags)
    for n, given in enumerate((h_flags, p_flags, q_flags, r_flags)):
        flags[n, :, pl.ds(0, 16)] = given[...].astype(F32)
    wides = [spread(8 * half) for half in (0, 1)]

    h_wides, p_wides = [
        [jnp.dot(flags[which], wide, preferred_element_type=F32) for wide in wides] for which in (0, 1)
    ]

    def masked(matrix, blocks, half, i):
        wide = blocks[half]
        return (matrix[pl.ds(i * B, B), pl.ds(half * T, T)].astype(F32) * wide[i : i + 1]).astype(BF)

    for half in (0, 1):
        for i in range(8):
            ps[me, half, pl.ds(i * B, B), :] = masked(den, p_wides, half, i)

    pl.semaphore_wait(barrier, 22 - mirror.astype(jnp.int32))

    pending = []

    def go(copy):
        copy.start()
        pending.append(copy)

    def got(dst, recv):
        remote(dst, dst, s_send.at[0], recv, core).wait_recv()

    AXES = (("y", "z"), ("z", "y"))
    OFFSET = (0, -1, 1, 2)

    def p_part(u, h, a, b, part):
        dy, dz = (a, b) if h == 0 else (b, a)
        s = ((y + dy) % 4) * 4 + (z + dz) % 4
        first, size = STREAMS[u][h]
        if part is not None:
            cut = (size // 2 + 15) // 16 * 16
            first, size = (first, cut) if part == 0 else (first + cut, size - cut)
        return ps.at[s, :, pl.ds(first, size), :]

    def p_go(u, h, a, b, part, axis, step, index):
        ref = p_part(u, h, a, b, part)
        go(remote(ref, ref, p_send.at[index], p_recv.at[index], near(axis, step)))

    def p_got(u, h, a, b, part, index):
        got(p_part(u, h, a, b, part), p_recv.at[index])

    def own(u, h):
        base = 40 * u + 20 * h
        p_go(u, h, 0, 0, None, AXES[h][0], 1, base)
        p_go(u, h, 0, 0, None, AXES[h][0], -1, base + 1)

    def pass_first(u, h, d):
        base, step = 40 * u + 20 * h, 1 - 2 * d
        p_got(u, h, -step, 0, None, base + d)
        p_go(u, h, -step, 0, d, AXES[h][0], step, base + 2 + d)

    def turn(u, h, j):
        base = 40 * u + 20 * h
        if j == 3:
            p_got(u, h, 2, 0, 0, base + 2)
            p_got(u, h, 2, 0, 1, base + 3)
        base += 4 + 4 * j
        p_go(u, h, OFFSET[j], 0, None, AXES[h][1], 1, base)
        p_go(u, h, OFFSET[j], 0, None, AXES[h][1], -1, base + 1)

    def pass_second(u, h, j, d):
        base, step = 40 * u + 20 * h + 4 + 4 * j, 1 - 2 * d
        p_got(u, h, OFFSET[j], -step, None, base + d)
        p_go(u, h, OFFSET[j], -step, d, AXES[h][1], step, base + 2 + d)

    def p_end(u, j):
        for h in (0, 1):
            base = 40 * u + 20 * h + 4 + 4 * j
            p_got(u, h, OFFSET[j], 2, 0, base + 2)
            p_got(u, h, OFFSET[j], 2, 1, base + 3)

    def h_part(step, c, p, part=None):
        first, size = (0, T) if part is None else (part * 256, 256)
        rows = pl.ds(pl.multiple_of(c * T + first, 256), size)
        return hs.at[((x + step) % 4) * 2 + (yh if p == 0 else 1 - yh), rows, :]

    def h_go(step, p, part, device, index):
        ref = h_part(step, k, p, part)
        go(remote(ref, ref, h_send.at[10 * p + index], h_recv.at[10 * p + index], device))

    def h_got(step, c, p, part, index):
        got(h_part(step, c, p, part), h_recv.at[10 * p + index])

    def h_swap():
        for half in (0, 1):
            for i in range(8):
                hm[half, pl.ds(i * B, B), :] = masked(ham, h_wides, half, i)
        go(remote(hm.at[1 - yh], h_part(0, k, 0), h_send.at[10], h_recv.at[10], across))
        h_local = pltpu.make_async_copy(hm.at[yh], h_part(0, k, 0), h_recv.at[0])
        h_local.start()
        h_local.wait()

    def h_start(p):
        if p == 1:
            h_got(0, k, 1, None, 0)
        h_go(0, p, None, near("x", 1), 2)
        h_go(0, p, None, near("x", -1), 3)
        h_go(0, p, None, core, 6)

    def h_pass(p, d):
        step = 1 - 2 * d
        h_got(-step, k, p, None, 2 + d)
        h_go(-step, p, d, near("x", step), 4 + d)
        h_go(-step, p, None, core, 7 + d)

    def h_end(p):
        h_got(2, k, p, 0, 4)
        h_got(2, k, p, 1, 5)
        h_go(2, p, None, core, 9)

    h_missing = [1]

    def h_ready():
        if h_missing:
            h_missing.clear()
            for p in (0, 1):
                for n, step in enumerate((0, -1, 1, 2)):
                    h_got(step, 1 - k, p, None, 6 + n)

    def pick(i, values):
        return sum(jnp.where(i == at, value, 0) for at, value in enumerate(values))

    def multiply_chips(u, chips):
        first, size = PARTS[u]
        rows = pl.ds(first, size)

        def body(i, carry):
            n = pick(i, chips)
            s = ((y + n // 4) % 2) * 4 + (z + n % 4) % 4
            left = jnp.concatenate(
                [jnp.concatenate([ps[s + 8 * c, half, rows, :] for half in (0, 1)], axis=1) for c in (0, 1)], axis=0
            )
            found = jnp.dot(left, hs[s], preferred_element_type=F32)
            for c in (0, 1):
                acc[c, rows, :] += found[c * size : (c + 1) * size]
            return carry

        lax.fori_loop(0, len(chips), body, 0)

    def multiply(u, g):
        h_ready()
        if g == 1:
            p_end(u, 0)
        elif g == 3:
            p_end(u, 1)
            p_end(u, 2)
        elif g == 4:
            p_end(u, 3)
        multiply_chips(u, ((4,), (0,), (5, 7), (1, 3, 6), (2,))[g])

    def f_part(u, step, c, j=None):
        first = ((x + step + plane + 2 * zl) % 4) * 4 + 2 * ((1 - c + zl) % 2)
        columns = pl.ds(*PARTS[u])
        return fs.at[pl.ds(first, 2), :, columns] if j is None else fs.at[first + j, :, columns]

    def f_go(u, step, j, device, index):
        ref = f_part(u, step, k, j)
        go(remote(ref, ref, f_send.at[10 * u + index], f_recv.at[10 * u + index], device))

    def f_got(u, step, c, j, index):
        got(f_part(u, step, c, j), f_recv.at[10 * u + index])

    def scatter(u):
        rows = pl.ds(*PARTS[u])
        for c in (0, 1):
            first = acc[c, rows, :] * qmask[c, rows, :].astype(F32)
            fb[c, rows, :] = first.astype(BF)
            ft[c, :, rows] = first.T.astype(BF)
            target = dev((y - x + 2 * c) % 4, 2 * k + xh, 2 * xl + c, (1 - zh + c) % 2)
            go(remote(ft.at[c, :, rows], fs.at[me, :, rows], f_send.at[10 * u + c], f_recv.at[10 * u + zl], target))

    def ring_start(u):
        for j in (0, 1):
            f_got(u, 0, k, j, j)
        f_go(u, 0, None, near("x", 1), 2)
        f_go(u, 0, None, near("x", -1), 3)
        f_go(u, 0, None, core, 6)

    def ring_pass(u, d):
        step = 1 - 2 * d
        f_got(u, -step, k, None, 2 + d)
        f_go(u, -step, d, near("x", step), 4 + d)
        f_go(u, -step, None, core, 7 + d)

    def ring_end(u):
        f_got(u, 2, k, 0, 4)
        f_got(u, 2, k, 1, 5)
        f_go(u, 2, None, core, 9)

    def multiply_second(v, which, places):
        rows, columns, size = pl.ds(*which), pl.ds(256 * v, 256), which[1]

        def body(n, carry):
            step = pick(n, [p[0] for p in places])
            c = pick(n, [p[1] for p in places])
            sy = (x + step + plane + 2 * zl) % 4
            sz = 2 * ((1 - c + zl) % 2)
            found = 0
            for j in (0, 1):
                s = (sy % 2) * 4 + sz + j
                left = jnp.concatenate([ps[s + 8 * half, sy // 2, rows, :] for half in (0, 1)], axis=0)
                found += jnp.dot(left, fs[sy * 4 + sz + j, :, columns], preferred_element_type=F32)
            for half in (0, 1):
                sums[half, rows, columns] += found[half * size : (half + 1) * size]
            return carry

        lax.fori_loop(0, len(places), body, 0)

    def second(v, g):
        if v == 0 and g < 2:
            if g == 0:
                f_got(0, 0, 1 - k, None, 6)
                multiply_second(0, (0, 256), [(0, k), (-1, k), (1, k), (0, 1 - k)])
            else:
                f_got(0, -1, 1 - k, None, 7)
                f_got(0, 1, 1 - k, None, 8)
                f_got(0, 2, 1 - k, None, 9)
                multiply_second(0, (0, 256), [(2, k), (-1, 1 - k), (1, 1 - k), (2, 1 - k)])
        elif v == 0:
            multiply_second(0, (256, 256), [(s, c) for s in OFFSET for c in (k, 1 - k)])
        elif g == 0:
            for u in range(1, N):
                f_got(u, 0, 1 - k, None, 6)
            multiply_second(1, (0, T), [(0, k), (-1, k), (1, k), (0, 1 - k)])
        else:
            for u in range(1, N):
                f_got(u, -1, 1 - k, None, 7)
                f_got(u, 1, 1 - k, None, 8)
                f_got(u, 2, 1 - k, None, 9)
            multiply_second(1, (0, T), [(2, k), (-1, 1 - k), (1, 1 - k), (2, 1 - k)])

    def columns_of(sy, sz, v):
        first = ((sy % 2) * 4 + sz) * 2 * T + (sy // 2) * T + 256 * v
        return pl.ds(pl.multiple_of(first, 256), 256)

    o_copy = []

    def finish(u):
        columns = pl.ds(256 * u, 256)
        for c in (0, 1):
            straight = fs[(2 * k + xh) * 4 + 2 * xl + c, :, columns].astype(F32)
            value = straight + fb[c, :, columns].astype(F32)
            gs[c, :, columns] = (value - sums[c, :, columns] * rmask[c, :, columns].astype(F32)).astype(BF)

        def rows_for(n):
            ty, tz = (y + n // 4) % 4, (z + n % 4) % 4
            b = (ty % 2) * 4 + tz
            return gs.at[ty // 2, pl.ds(pl.multiple_of(b * B, B), B), columns], dev(x, ty, tz, k)

        mine = out.at[:, columns_of(y, z, u)]
        local = pltpu.make_async_copy(rows_for(0)[0], mine, o_recv.at[16 * u + me])
        local.start()

        def copy(n):
            rows, device = rows_for(n)
            return remote(rows, mine, o_send.at[16 * u + n], o_recv.at[16 * u + me], device)

        def start(n, carry):
            copy(n).start()
            return carry

        lax.fori_loop(1, 16, start, 0)
        o_copy.append(copy)

    def masks():
        for n in (0, 1):
            got(qv.at[n], s_recv.at[n])
        got(rv.at[1 - yh], s_recv.at[2])
        eight = lax.broadcasted_iota(jnp.int32, (8, T), 0) == lax.broadcasted_iota(jnp.int32, (8, T), 1) // B
        narrow = spread(8 * yh)
        for c in (0, 1):
            qexp[...] = lax.dot_general(qv[c], eight.astype(F32), (((0,), (0,)), ((), ())), preferred_element_type=F32)
            q_wide = qexp[pl.ds(pl.multiple_of(k * 8, 8), 8), :]
            r_wide = 2.0 * jnp.dot(rv[c], narrow, preferred_element_type=F32)
            for i in range(8):
                qmask[c, pl.ds(i * B, B), :] = jnp.broadcast_to(q_wide[i : i + 1], (B, T)).astype(BF)
                rmask[c, pl.ds(i * B, B), :] = jnp.broadcast_to(r_wide[i : i + 1], (B, T)).astype(BF)

    own(0, 0); own(0, 1)
    rv[yh] = flags[3]
    q_copies = []
    for side in (0, 1):
        same = mirror & (k == side)
        copy = remote(
            flags.at[2], qv.at[zl], s_send.at[side], s_recv.at[zl],
            dev(2 * yl + zh, 2 * k + xh, 2 * xl + yh, side),
        )
        pl.when(jnp.logical_not(same))(copy.start)
        pl.when(same)(pltpu.make_async_copy(flags.at[2], qv.at[zl], s_recv.at[zl]).start)
        q_copies.append((same, copy))
    go(remote(rv.at[yh], rv.at[yh], s_send.at[2], s_recv.at[2], across))
    acc[...] = jnp.zeros_like(acc)
    sums[...] = jnp.zeros_like(sums)
    h_swap()
    h_start(0); turn(0, 1, 0); turn(0, 0, 0); pass_first(0, 1, 0); turn(0, 1, 1); pass_first(0, 1, 1)
    turn(0, 1, 2); pass_first(0, 0, 0); turn(0, 0, 1); pass_first(0, 0, 1); turn(0, 0, 2); pass_second(0, 0, 0, 0)
    pass_second(0, 0, 0, 1); h_pass(0, 0); h_pass(0, 1); turn(0, 1, 3); h_start(1); pass_second(0, 0, 1, 0)
    pass_second(0, 0, 1, 1); h_end(0); pass_second(0, 1, 0, 0); pass_second(0, 1, 0, 1); pass_second(0, 0, 2, 0)
    pass_second(0, 0, 2, 1); pass_second(0, 1, 1, 0); pass_second(0, 1, 1, 1); pass_second(0, 1, 2, 0)
    pass_second(0, 1, 2, 1); h_pass(1, 0); own(1, 0); turn(1, 0, 0); h_pass(1, 1); turn(0, 0, 3)
    masks()
    pass_second(1, 0, 0, 0); pass_second(1, 0, 0, 1); pass_second(0, 1, 3, 0); pass_second(0, 1, 3, 1); h_end(1)
    own(1, 1); turn(1, 1, 0); pass_second(0, 0, 3, 0); pass_second(0, 0, 3, 1)
    multiply(0, 0)
    multiply(0, 1)
    multiply(0, 2)
    pass_first(1, 1, 0); turn(1, 1, 1); pass_first(1, 1, 1); turn(1, 1, 2); pass_first(1, 0, 0); turn(1, 0, 1)
    pass_first(1, 0, 1); turn(1, 0, 2)
    multiply(0, 3)
    multiply(0, 4)
    scatter(0)
    turn(1, 1, 3); pass_second(1, 1, 0, 0); pass_second(1, 1, 0, 1)
    multiply(1, 0)
    pass_second(1, 0, 1, 0); pass_second(1, 0, 1, 1); pass_second(1, 1, 1, 0); pass_second(1, 1, 1, 1)
    pass_second(1, 0, 2, 0); pass_second(1, 0, 2, 1); pass_second(1, 1, 2, 0); pass_second(1, 1, 2, 1)
    turn(1, 0, 3); own(2, 0); turn(2, 0, 0); ring_start(0); own(2, 1); pass_second(1, 0, 3, 0)
    pass_second(1, 1, 3, 0); pass_second(1, 1, 3, 1); pass_second(1, 0, 3, 1); turn(2, 1, 0)
    multiply(1, 1)
    multiply(1, 2)
    pass_second(2, 0, 0, 0); pass_second(2, 0, 0, 1)
    multiply(1, 3)
    pass_first(2, 1, 0); turn(2, 1, 1); pass_first(2, 1, 1); turn(2, 1, 2); pass_first(2, 0, 0); turn(2, 0, 1)
    pass_first(2, 0, 1); turn(2, 0, 2)
    multiply(1, 4)
    scatter(1)
    turn(2, 1, 3); pass_second(2, 1, 0, 0); pass_second(2, 1, 0, 1)
    multiply(2, 0)
    pass_second(2, 0, 1, 0); ring_pass(0, 0); ring_pass(0, 1); pass_second(2, 0, 1, 1)
    second(0, 0)
    pass_second(2, 1, 1, 0); pass_second(2, 1, 1, 1); pass_second(2, 0, 2, 0); pass_second(2, 0, 2, 1)
    pass_second(2, 1, 2, 0); pass_second(2, 1, 2, 1); turn(2, 0, 3); ring_end(0); ring_start(1)
    pass_second(2, 1, 3, 0); pass_second(2, 1, 3, 1); pass_second(2, 0, 3, 0); pass_second(2, 0, 3, 1)
    multiply(2, 1)
    multiply(2, 2)
    second(0, 1)
    multiply(2, 3)
    multiply(2, 4)
    scatter(2)
    second(0, 2)
    ring_pass(1, 0); ring_pass(1, 1)
    finish(0)
    ring_start(2); ring_end(1); ring_pass(2, 0); ring_pass(2, 1)
    second(1, 0)
    ring_end(2)
    second(1, 1)
    finish(1)

    for u in (0, 1):
        def take(n, carry, u=u):
            got(out.at[:, columns_of(n // 4, n % 4, u)], o_recv.at[16 * u + n])
            return carry

        lax.fori_loop(0, 16, take, 0)
    for copy in pending:
        copy.wait_send()
    for same, copy in q_copies:
        pl.when(jnp.logical_not(same))(copy.wait_send)
    for copy in o_copy:
        def sent(n, carry, copy=copy):
            copy(n).wait_send()
            return carry

        lax.fori_loop(1, 16, sent, 0)


def per_device(hamiltonian, density, h_flags, p_flags, q_flags, r_flags):
    dma = pltpu.SemaphoreType.DMA
    rows = pl.pallas_call(
        kernel,
        out_shape=jax.ShapeDtypeStruct((64, 8192), BF),
        in_specs=[pl.BlockSpec(memory_space=pltpu.VMEM)] * 6,
        out_specs=pl.BlockSpec(memory_space=pl.ANY),
        scratch_shapes=[
            pltpu.VMEM((4, 8, 128), F32),
            pltpu.VMEM((16, 2, T, T), BF),
            pltpu.VMEM((8, 2 * T, T), BF),
            pltpu.VMEM((16, T, T), BF),
            pltpu.VMEM((2, T, T), BF),
            pltpu.VMEM((2, T, T), F32),
            pltpu.VMEM((2, T, T), F32),
            pltpu.VMEM((2, T, T), BF),
            pltpu.VMEM((2, T, T), BF),
            pltpu.VMEM((2, T, T), BF),
            pltpu.VMEM((2, 8, 128), F32),
            pltpu.VMEM((2, 8, 128), F32),
            pltpu.VMEM((2, T, T), BF),
            pltpu.VMEM((2, T, T), BF),
            pltpu.VMEM((128, T), F32),
            dma((40 * N,)), dma((40 * N,)), dma((20,)), dma((20,)), dma((10 * N,)), dma((10 * N,)),
            dma((3,)), dma((3,)), dma((32,)), dma((32,)),
        ],
        compiler_params=pltpu.CompilerParams(
            collective_id=0, has_side_effects=True, vmem_limit_bytes=60 * 1024 * 1024
        ),
        cost_estimate=pl.CostEstimate(flops=2 * 2 * 512 * 8192 * 1024, bytes_accessed=4 << 20, transcendentals=0),
    )(hamiltonian, density, h_flags, p_flags, q_flags, r_flags)
    return rows.astype(F32)


def solution(mesh):
    spec = P("row", "col")
    return jax.shard_map(
        per_device,
        mesh=mesh,
        in_specs=(spec,) * 6,
        out_specs=P(("row", "col"), None),
        check_vma=False,
    )
```

```python
import jax
import jax.numpy as jnp
from jax import lax
from jax.experimental import pallas as pl
from jax.experimental.pallas import tpu as pltpu
from jax.sharding import PartitionSpec as P

MESH = pl.DeviceIdType.MESH
BF = jnp.bfloat16
F32 = jnp.float32
B = 64
T = 512
PARTS = ((0, 256), (256, 128), (384, 128))
STREAMS = (((0, 144), (144, 112)), ((256, 64), (320, 64)), ((384, 64), (448, 64)))
N = len(PARTS)


def dev(x, y, z, k):
    return (x * 4 + (y // 2) * 2 + k, (y % 2) * 4 + z)


def kernel(
    ham, den, h_flags, p_flags, q_flags, r_flags, out,
    flags, ps, hs, fs, hm, acc, sums, fb, ft, gs, qv, rv, qmask, rmask, qexp,
    p_send, p_recv, h_send, h_recv, f_send, f_recv, s_send, s_recv, o_send, o_recv,
):
    row, col = lax.axis_index("row"), lax.axis_index("col")
    x, yh, k = row // 4, (row // 2) % 2, row % 2
    yl, z = col // 4, col % 4
    y = yh * 2 + yl
    zh, zl = z // 2, z % 2
    xh, xl = x // 2, x % 2
    me = y * 4 + z
    plane = 2 * yl + zh

    def near(axis, step):
        if axis == "x":
            return dev((x + step) % 4, y, z, k)
        if axis == "y":
            return dev(x, (y + step) % 4, z, k)
        return dev(x, y, (z + step) % 4, k)

    core = dev(x, y, z, 1 - k)
    across = near("y", 2)

    def remote(src, dst, send, recv, device):
        return pltpu.make_async_remote_copy(
            src_ref=src, dst_ref=dst, send_sem=send, recv_sem=recv,
            device_id=device, device_id_type=MESH,
        )

    barrier = pltpu.get_barrier_semaphore()

    def greet(device):
        pl.semaphore_signal(barrier, inc=1, device_id=device, device_id_type=MESH)

    def greet_plane(n, carry):
        greet(dev(x, (y + n // 4) % 4, (z + n % 4) % 4, k))
        return carry

    lax.fori_loop(1, 16, greet_plane, 0)
    greet(near("x", 1))
    greet(near("x", -1))
    greet(core)
    for j in (0, 1):
        greet(dev(plane, (x + plane + 2 * zl) % 4, 2 * ((1 - k + zl) % 2) + j, yh))
    mirror = (x == plane) & (y == 2 * k + xh) & (z == 2 * xl + yh)
    for c in (0, 1):
        pl.when(jnp.logical_not(mirror & (zl == c)))(
            lambda c=c: greet(dev(plane, 2 * zl + xh, 2 * xl + c, yh))
        )

    def spread(first):
        blocks = lax.broadcasted_iota(jnp.int32, (128, T), 0)
        places = lax.broadcasted_iota(jnp.int32, (128, T), 1) // B
        return (blocks == places + first).astype(F32)

    flags[...] = jnp.zeros_like(flags)
    for n, given in enumerate((h_flags, p_flags, q_flags, r_flags)):
        flags[n, :, pl.ds(0, 16)] = given[...].astype(F32)
    wides = [spread(8 * half) for half in (0, 1)]

    h_wides, p_wides = [
        [jnp.dot(flags[which], wide, preferred_element_type=F32) for wide in wides] for which in (0, 1)
    ]

    def masked(matrix, blocks, half, i):
        wide = blocks[half]
        return (matrix[pl.ds(i * B, B), pl.ds(half * T, T)].astype(F32) * wide[i : i + 1]).astype(BF)

    for half in (0, 1):
        for i in range(8):
            ps[me, half, pl.ds(i * B, B), :] = masked(den, p_wides, half, i)

    pl.semaphore_wait(barrier, 22 - mirror.astype(jnp.int32))

    pending = []

    def go(copy):
        copy.start()
        pending.append(copy)

    def got(dst, recv):
        remote(dst, dst, s_send.at[0], recv, core).wait_recv()

    AXES = (("y", "z"), ("z", "y"))
    OFFSET = (0, -1, 1, 2)

    def p_part(u, h, a, b, part):
        dy, dz = (a, b) if h == 0 else (b, a)
        s = ((y + dy) % 4) * 4 + (z + dz) % 4
        first, size = STREAMS[u][h]
        if part is not None:
            cut = (size // 2 + 15) // 16 * 16
            first, size = (first, cut) if part == 0 else (first + cut, size - cut)
        return ps.at[s, :, pl.ds(first, size), :]

    def p_go(u, h, a, b, part, axis, step, index):
        ref = p_part(u, h, a, b, part)
        go(remote(ref, ref, p_send.at[index], p_recv.at[index], near(axis, step)))

    def p_got(u, h, a, b, part, index):
        got(p_part(u, h, a, b, part), p_recv.at[index])

    def own(u, h):
        base = 40 * u + 20 * h
        p_go(u, h, 0, 0, None, AXES[h][0], 1, base)
        p_go(u, h, 0, 0, None, AXES[h][0], -1, base + 1)

    def pass_first(u, h, d):
        base, step = 40 * u + 20 * h, 1 - 2 * d
        p_got(u, h, -step, 0, None, base + d)
        p_go(u, h, -step, 0, d, AXES[h][0], step, base + 2 + d)

    def turn(u, h, j):
        base = 40 * u + 20 * h
        if j == 3:
            p_got(u, h, 2, 0, 0, base + 2)
            p_got(u, h, 2, 0, 1, base + 3)
        base += 4 + 4 * j
        p_go(u, h, OFFSET[j], 0, None, AXES[h][1], 1, base)
        p_go(u, h, OFFSET[j], 0, None, AXES[h][1], -1, base + 1)

    def pass_second(u, h, j, d):
        base, step = 40 * u + 20 * h + 4 + 4 * j, 1 - 2 * d
        p_got(u, h, OFFSET[j], -step, None, base + d)
        p_go(u, h, OFFSET[j], -step, d, AXES[h][1], step, base + 2 + d)

    def p_end(u, j):
        for h in (0, 1):
            base = 40 * u + 20 * h + 4 + 4 * j
            p_got(u, h, OFFSET[j], 2, 0, base + 2)
            p_got(u, h, OFFSET[j], 2, 1, base + 3)

    def h_part(step, c, p, part=None):
        first, size = (0, T) if part is None else (part * 256, 256)
        rows = pl.ds(pl.multiple_of(c * T + first, 256), size)
        return hs.at[((x + step) % 4) * 2 + (yh if p == 0 else 1 - yh), rows, :]

    def h_go(step, p, part, device, index):
        ref = h_part(step, k, p, part)
        go(remote(ref, ref, h_send.at[10 * p + index], h_recv.at[10 * p + index], device))

    def h_got(step, c, p, part, index):
        got(h_part(step, c, p, part), h_recv.at[10 * p + index])

    def h_swap():
        for half in (0, 1):
            for i in range(8):
                hm[half, pl.ds(i * B, B), :] = masked(ham, h_wides, half, i)
        go(remote(hm.at[1 - yh], h_part(0, k, 0), h_send.at[10], h_recv.at[10], across))
        h_local = pltpu.make_async_copy(hm.at[yh], h_part(0, k, 0), h_recv.at[0])
        h_local.start()
        h_local.wait()

    def h_start(p):
        if p == 1:
            h_got(0, k, 1, None, 0)
        h_go(0, p, None, near("x", 1), 2)
        h_go(0, p, None, near("x", -1), 3)
        h_go(0, p, None, core, 6)

    def h_pass(p, d):
        step = 1 - 2 * d
        h_got(-step, k, p, None, 2 + d)
        h_go(-step, p, d, near("x", step), 4 + d)
        h_go(-step, p, None, core, 7 + d)

    def h_end(p):
        h_got(2, k, p, 0, 4)
        h_got(2, k, p, 1, 5)
        h_go(2, p, None, core, 9)

    h_missing = [1]

    def h_ready():
        if h_missing:
            h_missing.clear()
            for p in (0, 1):
                for n, step in enumerate((0, -1, 1, 2)):
                    h_got(step, 1 - k, p, None, 6 + n)

    def pick(i, values):
        return sum(jnp.where(i == at, value, 0) for at, value in enumerate(values))

    def multiply_chips(u, chips):
        first, size = PARTS[u]
        rows = pl.ds(first, size)

        def body(i, carry):
            n = pick(i, chips)
            s = ((y + n // 4) % 2) * 4 + (z + n % 4) % 4
            left = jnp.concatenate(
                [jnp.concatenate([ps[s + 8 * c, half, rows, :] for half in (0, 1)], axis=1) for c in (0, 1)], axis=0
            )
            found = jnp.dot(left, hs[s], preferred_element_type=F32)
            for c in (0, 1):
                acc[c, rows, :] += found[c * size : (c + 1) * size]
            return carry

        lax.fori_loop(0, len(chips), body, 0)

    def multiply(u, g):
        h_ready()
        if g == 1:
            p_end(u, 0)
        elif g == 3:
            p_end(u, 1)
            p_end(u, 2)
        elif g == 4:
            p_end(u, 3)
        multiply_chips(u, ((4,), (0,), (5, 7), (1, 3, 6), (2,))[g])

    def f_part(u, step, c, j=None):
        first = ((x + step + plane + 2 * zl) % 4) * 4 + 2 * ((1 - c + zl) % 2)
        columns = pl.ds(*PARTS[u])
        return fs.at[pl.ds(first, 2), :, columns] if j is None else fs.at[first + j, :, columns]

    def f_go(u, step, j, device, index):
        ref = f_part(u, step, k, j)
        go(remote(ref, ref, f_send.at[10 * u + index], f_recv.at[10 * u + index], device))

    def f_got(u, step, c, j, index):
        got(f_part(u, step, c, j), f_recv.at[10 * u + index])

    def scatter(u):
        rows = pl.ds(*PARTS[u])
        for c in (0, 1):
            first = acc[c, rows, :] * qmask[c, rows, :].astype(F32)
            fb[c, rows, :] = first.astype(BF)
            ft[c, :, rows] = first.T.astype(BF)
            target = dev((y - x + 2 * c) % 4, 2 * k + xh, 2 * xl + c, (1 - zh + c) % 2)
            go(remote(ft.at[c, :, rows], fs.at[me, :, rows], f_send.at[10 * u + c], f_recv.at[10 * u + zl], target))

    def ring_start(u):
        for j in (0, 1):
            f_got(u, 0, k, j, j)
        f_go(u, 0, None, near("x", 1), 2)
        f_go(u, 0, None, near("x", -1), 3)
        f_go(u, 0, None, core, 6)

    def ring_pass(u, d):
        step = 1 - 2 * d
        f_got(u, -step, k, None, 2 + d)
        f_go(u, -step, d, near("x", step), 4 + d)
        f_go(u, -step, None, core, 7 + d)

    def ring_end(u):
        f_got(u, 2, k, 0, 4)
        f_got(u, 2, k, 1, 5)
        f_go(u, 2, None, core, 9)

    def multiply_second(v, which, places):
        rows, columns, size = pl.ds(*which), pl.ds(256 * v, 256), which[1]

        def body(n, carry):
            step = pick(n, [p[0] for p in places])
            c = pick(n, [p[1] for p in places])
            sy = (x + step + plane + 2 * zl) % 4
            sz = 2 * ((1 - c + zl) % 2)
            found = 0
            for j in (0, 1):
                s = (sy % 2) * 4 + sz + j
                left = jnp.concatenate([ps[s + 8 * half, sy // 2, rows, :] for half in (0, 1)], axis=0)
                found += jnp.dot(left, fs[sy * 4 + sz + j, :, columns], preferred_element_type=F32)
            for half in (0, 1):
                sums[half, rows, columns] += found[half * size : (half + 1) * size]
            return carry

        lax.fori_loop(0, len(places), body, 0)

    def second(v, g):
        if v == 0 and g < 2:
            if g == 0:
                f_got(0, 0, 1 - k, None, 6)
                multiply_second(0, (0, 256), [(0, k), (-1, k), (1, k), (0, 1 - k)])
            else:
                f_got(0, -1, 1 - k, None, 7)
                f_got(0, 1, 1 - k, None, 8)
                f_got(0, 2, 1 - k, None, 9)
                multiply_second(0, (0, 256), [(2, k), (-1, 1 - k), (1, 1 - k), (2, 1 - k)])
        elif v == 0:
            multiply_second(0, (256, 256), [(s, c) for s in OFFSET for c in (k, 1 - k)])
        elif g == 0:
            for u in range(1, N):
                f_got(u, 0, 1 - k, None, 6)
            multiply_second(1, (0, T), [(0, k), (-1, k), (1, k), (0, 1 - k)])
        else:
            for u in range(1, N):
                f_got(u, -1, 1 - k, None, 7)
                f_got(u, 1, 1 - k, None, 8)
                f_got(u, 2, 1 - k, None, 9)
            multiply_second(1, (0, T), [(2, k), (-1, 1 - k), (1, 1 - k), (2, 1 - k)])

    def columns_of(sy, sz, v):
        first = ((sy % 2) * 4 + sz) * 2 * T + (sy // 2) * T + 256 * v
        return pl.ds(pl.multiple_of(first, 256), 256)

    o_copy = []

    def finish(u):
        columns = pl.ds(256 * u, 256)
        for c in (0, 1):
            straight = fs[(2 * k + xh) * 4 + 2 * xl + c, :, columns].astype(F32)
            value = straight + fb[c, :, columns].astype(F32)
            gs[c, :, columns] = (value - sums[c, :, columns] * rmask[c, :, columns].astype(F32)).astype(BF)

        def rows_for(n):
            ty, tz = (y + n // 4) % 4, (z + n % 4) % 4
            b = (ty % 2) * 4 + tz
            return gs.at[ty // 2, pl.ds(pl.multiple_of(b * B, B), B), columns], dev(x, ty, tz, k)

        mine = out.at[:, columns_of(y, z, u)]
        local = pltpu.make_async_copy(rows_for(0)[0], mine, o_recv.at[16 * u + me])
        local.start()

        def copy(n):
            rows, device = rows_for(n)
            return remote(rows, mine, o_send.at[16 * u + n], o_recv.at[16 * u + me], device)

        def start(n, carry):
            copy(n).start()
            return carry

        lax.fori_loop(1, 16, start, 0)
        o_copy.append(copy)

    def masks():
        for n in (0, 1):
            got(qv.at[n], s_recv.at[n])
        got(rv.at[1 - yh], s_recv.at[2])
        eight = lax.broadcasted_iota(jnp.int32, (8, T), 0) == lax.broadcasted_iota(jnp.int32, (8, T), 1) // B
        narrow = spread(8 * yh)
        for c in (0, 1):
            qexp[...] = lax.dot_general(qv[c], eight.astype(F32), (((0,), (0,)), ((), ())), preferred_element_type=F32)
            q_wide = qexp[pl.ds(pl.multiple_of(k * 8, 8), 8), :]
            r_wide = 2.0 * jnp.dot(rv[c], narrow, preferred_element_type=F32)
            for i in range(8):
                qmask[c, pl.ds(i * B, B), :] = jnp.broadcast_to(q_wide[i : i + 1], (B, T)).astype(BF)
                rmask[c, pl.ds(i * B, B), :] = jnp.broadcast_to(r_wide[i : i + 1], (B, T)).astype(BF)

    own(0, 0); own(0, 1); turn(0, 1, 0)
    rv[yh] = flags[3]
    q_copies = []
    for side in (0, 1):
        same = mirror & (k == side)
        copy = remote(
            flags.at[2], qv.at[zl], s_send.at[side], s_recv.at[zl],
            dev(2 * yl + zh, 2 * k + xh, 2 * xl + yh, side),
        )
        pl.when(jnp.logical_not(same))(copy.start)
        pl.when(same)(pltpu.make_async_copy(flags.at[2], qv.at[zl], s_recv.at[zl]).start)
        q_copies.append((same, copy))
    go(remote(rv.at[yh], rv.at[yh], s_send.at[2], s_recv.at[2], across))
    acc[...] = jnp.zeros_like(acc)
    sums[...] = jnp.zeros_like(sums)
    h_swap()
    h_start(0); turn(0, 0, 0); pass_first(0, 1, 0); turn(0, 1, 1); pass_first(0, 1, 1); turn(0, 1, 2)
    pass_first(0, 0, 0); pass_first(0, 0, 1); turn(0, 0, 1); turn(0, 0, 2); pass_second(0, 1, 0, 0)
    pass_second(0, 1, 0, 1); pass_second(0, 0, 0, 0); pass_second(0, 0, 0, 1); h_pass(0, 0); h_pass(0, 1)
    turn(0, 1, 3); pass_second(0, 0, 1, 0); pass_second(0, 0, 1, 1); h_end(0); h_start(1); pass_second(0, 0, 2, 0)
    pass_second(0, 0, 2, 1); pass_second(0, 1, 1, 0); pass_second(0, 1, 1, 1); own(1, 0); turn(1, 0, 0)
    pass_second(0, 1, 2, 0); pass_second(0, 1, 2, 1); own(1, 1); turn(1, 1, 0); turn(0, 0, 3)
    masks()
    h_pass(1, 0); h_pass(1, 1); pass_second(1, 0, 0, 0); pass_second(1, 0, 0, 1); pass_first(1, 1, 0)
    turn(1, 1, 1); pass_first(1, 1, 1); turn(1, 1, 2); pass_second(0, 1, 3, 0); pass_second(0, 1, 3, 1); own(2, 0)
    turn(2, 0, 0); pass_second(0, 0, 3, 0); pass_second(0, 0, 3, 1); pass_first(1, 0, 0); pass_first(1, 0, 1)
    turn(1, 0, 1); turn(1, 0, 2); h_end(1); turn(1, 1, 3); pass_second(1, 1, 0, 0); pass_second(1, 1, 0, 1)
    pass_second(2, 0, 0, 0); pass_second(2, 0, 0, 1)
    multiply(0, 0)
    multiply(0, 1)
    pass_second(1, 1, 1, 0); pass_second(1, 1, 1, 1)
    multiply(0, 2)
    multiply(0, 3)
    pass_second(1, 0, 1, 0); pass_second(1, 0, 1, 1); pass_second(1, 1, 2, 0); pass_second(1, 1, 2, 1)
    multiply(1, 0)
    own(2, 1)
    multiply(0, 4)
    scatter(0)
    pass_second(1, 0, 2, 0); pass_second(1, 0, 2, 1); pass_first(2, 0, 0); turn(2, 0, 1); pass_first(2, 0, 1)
    turn(2, 0, 2); turn(2, 1, 0); turn(1, 0, 3); pass_first(2, 1, 0); turn(2, 1, 1); pass_second(1, 1, 3, 0)
    pass_second(1, 1, 3, 1); pass_first(2, 1, 1); turn(2, 1, 2)
    multiply(1, 1)
    multiply(1, 2)
    pass_second(2, 0, 1, 0); pass_second(2, 0, 1, 1); turn(2, 0, 3); ring_start(0); pass_second(2, 0, 2, 0)
    pass_second(2, 0, 2, 1); pass_second(2, 1, 0, 0); pass_second(2, 1, 0, 1)
    multiply(2, 0)
    pass_second(1, 0, 3, 0); pass_second(1, 0, 3, 1)
    multiply(1, 3)
    turn(2, 1, 3); pass_second(2, 1, 1, 0); pass_second(2, 1, 1, 1); pass_second(2, 0, 3, 0)
    pass_second(2, 0, 3, 1); pass_second(2, 1, 2, 0); pass_second(2, 1, 2, 1)
    multiply(2, 1)
    multiply(2, 2)
    multiply(1, 4)
    scatter(1)
    pass_second(2, 1, 3, 0); pass_second(2, 1, 3, 1); ring_pass(0, 0); ring_pass(0, 1)
    second(0, 0)
    multiply(2, 3)
    multiply(2, 4)
    scatter(2)
    ring_start(1); ring_end(0); ring_start(2)
    second(0, 1)
    second(0, 2)
    ring_pass(1, 1); ring_pass(1, 0)
    finish(0)
    ring_pass(2, 0); ring_pass(2, 1)
    second(1, 0)
    ring_end(1); ring_end(2)
    second(1, 1)
    finish(1)

    for u in (0, 1):
        def take(n, carry, u=u):
            got(out.at[:, columns_of(n // 4, n % 4, u)], o_recv.at[16 * u + n])
            return carry

        lax.fori_loop(0, 16, take, 0)
    for copy in pending:
        copy.wait_send()
    for same, copy in q_copies:
        pl.when(jnp.logical_not(same))(copy.wait_send)
    for copy in o_copy:
        def sent(n, carry, copy=copy):
            copy(n).wait_send()
            return carry

        lax.fori_loop(1, 16, sent, 0)


def per_device(hamiltonian, density, h_flags, p_flags, q_flags, r_flags):
    dma = pltpu.SemaphoreType.DMA
    rows = pl.pallas_call(
        kernel,
        out_shape=jax.ShapeDtypeStruct((64, 8192), BF),
        in_specs=[pl.BlockSpec(memory_space=pltpu.VMEM)] * 6,
        out_specs=pl.BlockSpec(memory_space=pl.ANY),
        scratch_shapes=[
            pltpu.VMEM((4, 8, 128), F32),
            pltpu.VMEM((16, 2, T, T), BF),
            pltpu.VMEM((8, 2 * T, T), BF),
            pltpu.VMEM((16, T, T), BF),
            pltpu.VMEM((2, T, T), BF),
            pltpu.VMEM((2, T, T), F32),
            pltpu.VMEM((2, T, T), F32),
            pltpu.VMEM((2, T, T), BF),
            pltpu.VMEM((2, T, T), BF),
            pltpu.VMEM((2, T, T), BF),
            pltpu.VMEM((2, 8, 128), F32),
            pltpu.VMEM((2, 8, 128), F32),
            pltpu.VMEM((2, T, T), BF),
            pltpu.VMEM((2, T, T), BF),
            pltpu.VMEM((128, T), F32),
            dma((40 * N,)), dma((40 * N,)), dma((20,)), dma((20,)), dma((10 * N,)), dma((10 * N,)),
            dma((3,)), dma((3,)), dma((32,)), dma((32,)),
        ],
        compiler_params=pltpu.CompilerParams(
            collective_id=0, has_side_effects=True, vmem_limit_bytes=60 * 1024 * 1024
        ),
        cost_estimate=pl.CostEstimate(flops=2 * 2 * 512 * 8192 * 1024, bytes_accessed=4 << 20, transcendentals=0),
    )(hamiltonian, density, h_flags, p_flags, q_flags, r_flags)
    return rows.astype(F32)


def solution(mesh):
    spec = P("row", "col")
    return jax.shard_map(
        per_device,
        mesh=mesh,
        in_specs=(spec,) * 6,
        out_specs=P(("row", "col"), None),
        check_vma=False,
    )
```
